256 devices in a mesh: dp: 4 (over x), ctx: 64 (over y, z, core).
Axes of the slice: x: 4, y: 4, z: 8, core: 2. Of those that a mesh axis runs over, the one named last changes fastest.
Arguments:
- video_query: bfloat16 [4, 8192, 3072], P('dp', 'ctx'), may hold values from -80 to 80
- video_key: bfloat16 [4, 8192, 3072], P('dp', 'ctx'), may hold values from -6 to 6
- video_value: bfloat16 [4, 8192, 3072], P('dp', 'ctx'), may hold values from -6 to 6
- audio_key: bfloat16 [4, 1024, 3072], P('dp', 'ctx'), may hold values from -6 to 6
- audio_value: bfloat16 [4, 1024, 3072], P('dp', 'ctx'), may hold values from -6 to 6
- cross_gate: float32 [3072], replicated, may hold values from -6 to 6
- out_cotangent: bfloat16 [4, 8192, 3072], P('dp', 'ctx'), may hold values from -6 to 6
- tile_list: int32 [128, 4], replicated, may hold values from 0 to 127, as said below
- tile_count: int32 [128], replicated, may hold values from 2 to 4, as said below
- audio_list: int32 [128, 2], replicated, may hold values from 0 to 63, as said below
Outputs:
- query_grad: bfloat16 [4, 8192, 3072], P('dp', 'ctx')
- key_grad: bfloat16 [4, 8192, 3072], P('dp', 'ctx')
- value_grad: bfloat16 [4, 8192, 3072], P('dp', 'ctx')
- audio_key_grad: bfloat16 [4, 1024, 3072], P('dp', 'ctx')
- audio_value_grad: bfloat16 [4, 1024, 3072], P('dp', 'ctx')
- gate_grad: float32 [3072], replicated
The draws below stay inside these ranges and needn't reach their ends.
Inputs may be any that keep to these rules, and one draw needn't show every extreme that they name: `tile_list`: entry 0 of row t is t itself; every entry lies in tiles (t // 2 - 1) * 2 to (t // 2 + 2) * 2 - 1; the first tile_count[t] entries are distinct, the others are padding. `tile_count`: live slots of row t of tile_list. `audio_list`: entry 0 of row t is block t // 2, aligned with the tile in time; entry 1 is a block next to it.
All inputs are finite; a program needn't handle non-finite values.
Results may differ from the reference program's by a relative error of at most 0.015.
Values may be sent and summed in bfloat16 or wider, within the bound.
No kernel may reach another device: no remote copies, remote signals or barrier semaphores. Data moves between devices by JAX's collectives and lax.ppermute only.
A program may use at most 128 MiB of HBM per device.

```python
import math
import jax
import jax.numpy as jnp
from jax import lax

HEADS = 24
HEAD_DIM = 128
DIM = 3072
TILE = 64
KB = 4
KA = 2
TV_DEV = 128
TA_DEV = 16
TILES_DEV = 2
CLIPS = 4
TV = 8192
TA = 1024
TILES = 128
N_CTX = 64


def blended_field(key, shape):
    normal_part = jnp.clip(jax.random.normal(jax.random.fold_in(key, 1), shape), -6.0, 6.0)
    return normal_part


def shared_keys(key, flat_share):
    base_field = blended_field(jax.random.fold_in(key, 5), (CLIPS, TV, DIM))
    strength = 120.0 * 4.0 ** jax.random.uniform(jax.random.fold_in(key, 6), (CLIPS, TV, 1))
    row_index = jnp.arange(TV)[None, :, None]
    follower = (row_index % TILE == 1) & (flat_share > 0.0)
    earlier = jnp.roll(base_field, 1, axis=1)
    earlier_strength = jnp.roll(strength, 1, axis=1)
    key_field = jnp.where(follower, earlier * (1.0 - 2.0 / earlier_strength), base_field)
    return (jnp.clip(key_field, -6.0, 6.0), strength)


def draw_video_key(key, part):
    flat_share = 0.0
    key_field, strength = shared_keys(key, flat_share)
    return key_field.astype(jnp.bfloat16)


def draw_video_query(key, part):
    flat_share = 0.0
    key_field, strength = shared_keys(key, flat_share)
    key = jax.random.fold_in(key, 32)
    own_field = blended_field(key, (CLIPS, TV, DIM))
    row_index = jnp.arange(TV)[None, :, None]
    leader = (row_index % TILE == 0) & (flat_share > 0.0)
    queries = jnp.where(leader, key_field * strength / math.sqrt(HEAD_DIM), own_field)
    return jnp.clip(queries, -80.0, 80.0).astype(jnp.bfloat16)


def draw_audio_key(key, part):
    flat_share = 0.0
    key_field, strength = shared_keys(key, flat_share)
    key = jax.random.fold_in(key, 33)
    own_field = blended_field(key, (CLIPS, TA, DIM))
    audio_index = jnp.arange(TA)
    source_rows = audio_index * 8
    prior_rows = jnp.maximum(audio_index - 1, 0) * 8
    aligned = (source_rows % TILE == 0) & (flat_share > 0.0)
    trailing = (prior_rows % TILE == 0) & (audio_index >= 1) & (flat_share > 0.0)
    copied = key_field[:, source_rows]
    prior = key_field[:, prior_rows] * (1.0 - 2.0 / strength[:, prior_rows])
    audio_field = jnp.where(aligned[None, :, None], copied, jnp.where(trailing[None, :, None], prior, own_field))
    return jnp.clip(audio_field, -6.0, 6.0).astype(jnp.bfloat16)


def draw_tile_list(key, part):
    key = jax.random.fold_in(key, 41)
    tile_index = jnp.arange(TILES, dtype=jnp.int32)[:, None]
    holder = tile_index // TILES_DEV
    offset = jnp.arange(3 * TILES_DEV, dtype=jnp.int32)[None, :]
    candidate = (holder - 1) * TILES_DEV + offset
    usable = (candidate >= 0) & (candidate < TILES) & (candidate != tile_index)
    random_part = jax.random.randint(key, (TILES, 3 * TILES_DEV), 0, 2 ** 20, dtype=jnp.int32)
    ranking = jnp.where(candidate == tile_index, 2 ** 30, jnp.where(usable, random_part * (4 * TILES_DEV) + offset, -1 - offset))
    chosen_rank, chosen = lax.top_k(ranking, KB)
    picked = jnp.take_along_axis(candidate, chosen, axis=1)
    return jnp.where(chosen_rank >= 0, picked, tile_index).astype(jnp.int32)


def draw_tile_count(key, part):
    key = jax.random.fold_in(key, 42)
    tile_index = jnp.arange(TILES, dtype=jnp.int32)
    drawn = jax.random.randint(key, (TILES,), KB // 2, KB + 1, dtype=jnp.int32)
    return jnp.where(tile_index % TILES_DEV == 0, KB, drawn).astype(jnp.int32)


def draw_audio_list(key, part):
    key = jax.random.fold_in(key, 43)
    block_total = TILES // TILES_DEV
    holder = jnp.arange(TILES, dtype=jnp.int32) // TILES_DEV
    side_step = jax.random.randint(key, (TILES,), 0, 2, dtype=jnp.int32) * 2 - 1
    neighbour = holder + side_step
    neighbour = jnp.where(neighbour < 0, 1, jnp.where(neighbour >= block_total, block_total - 2, neighbour))
    return jnp.stack((holder, neighbour), axis=1).astype(jnp.int32)


def shard_levels(stream_key, shape, cuts, least, largest):
    loudness = 1.0
    for axis_at, shards_of in cuts:
        heights = jax.random.uniform(jax.random.fold_in(jax.random.fold_in(stream_key, 6), axis_at), (shards_of,), jnp.float32, least / len(cuts), largest / len(cuts))
        loudness = loudness * jnp.repeat(jnp.exp(heights), shape[axis_at] // shards_of).reshape((-1,) + (1,) * (len(shape) - 1 - axis_at))
    return loudness


def normal_values(stream_key, dims, spread, reach, cuts=(), kind=jnp.bfloat16):
    factor_of = shard_levels(stream_key, dims, cuts, -0.22, 0.18) if cuts else 1.0
    values = jax.random.normal(stream_key, dims, jnp.float32) * spread * factor_of
    return jnp.minimum(jnp.maximum(values, -reach), reach).astype(kind)


def setup_inputs(seed: int = 0) -> dict:
    seeds = jax.random.split(jax.random.key(seed), 11)
    return {
        "video_query": draw_video_query(jax.random.fold_in(seeds[10], 71), 0),
        "video_key": draw_video_key(jax.random.fold_in(seeds[10], 71), 0),
        "video_value": normal_values(seeds[2], (CLIPS, TV, DIM), 1.0, 6.0, ((0, 4), (1, 64))),
        "audio_key": draw_audio_key(jax.random.fold_in(seeds[10], 71), 0),
        "audio_value": normal_values(seeds[4], (CLIPS, TA, DIM), 1.0, 6.0, ((0, 4), (1, 64))),
        "cross_gate": normal_values(seeds[5], (DIM,), 1.0, 6.0, (), jnp.float32),
        "out_cotangent": normal_values(seeds[6], (CLIPS, TV, DIM), 1.0, 6.0, ((0, 4), (1, 64))),
        "tile_list": draw_tile_list(jax.random.fold_in(seeds[10], 71), 0),
        "tile_count": draw_tile_count(jax.random.fold_in(seeds[10], 71), 0),
        "audio_list": draw_audio_list(jax.random.fold_in(seeds[10], 71), 0),
    }


def split_heads(array):
    return array.reshape(array.shape[:-1] + (HEADS, HEAD_DIM)).astype(jnp.float32)

def rounded(array):
    return lax.optimization_barrier(array.astype(jnp.bfloat16)).astype(jnp.float32)

def gather_slots(window, slot_ids):
    picked = jnp.take(window, slot_ids, axis=1)
    return picked.reshape(picked.shape[0], slot_ids.shape[0], slot_ids.shape[1] * window.shape[2], window.shape[3])

def key_scores(queries, key_rows, key_mask):
    score_scale = 1.0 / math.sqrt(HEAD_DIM)
    scores = jnp.einsum('cnlhe,cnkhe->cnhlk', split_heads(queries), split_heads(key_rows)) * score_scale
    return jnp.where(key_mask[None, :, None, None, :], scores, -jnp.inf)

def attend(queries, key_rows, value_rows, key_mask):
    scores = key_scores(queries, key_rows, key_mask)
    row_top = lax.optimization_barrier(jnp.max(scores, axis=-1, keepdims=True))
    log_total = row_top + jnp.log(lax.optimization_barrier(jnp.sum(jnp.exp(scores - row_top), axis=-1, keepdims=True)))
    weights = rounded(jnp.exp(scores - log_total))
    mixed = jnp.einsum('cnhlk,cnkhe->cnlhe', weights, split_heads(value_rows))
    return (mixed.reshape(queries.shape), log_total[..., 0])

def head_sums(cotangent, mixed):
    product = split_heads(cotangent.astype(jnp.float32) * mixed)
    return jnp.swapaxes(lax.optimization_barrier(jnp.sum(product, axis=-1)), -1, -2)

def attend_back(queries, cotangent, key_rows, value_rows, key_mask, log_total, row_delta):
    score_scale = 1.0 / math.sqrt(HEAD_DIM)
    probabilities = jnp.exp(key_scores(queries, key_rows, key_mask) - log_total[..., None])
    weights = rounded(probabilities)
    split_cotangent = split_heads(cotangent)
    prob_grads = jnp.einsum('cnlhe,cnkhe->cnhlk', split_cotangent, split_heads(value_rows))
    score_grads = rounded(probabilities * (prob_grads - row_delta[..., None]))
    grad_query = jnp.einsum('cnhlk,cnkhe->cnlhe', score_grads, split_heads(key_rows)) * score_scale
    grad_key = jnp.einsum('cnhlk,cnlhe->cnkhe', score_grads, split_heads(queries)) * score_scale
    grad_value = jnp.einsum('cnhlk,cnlhe->cnkhe', weights, split_cotangent)
    return (grad_query.reshape(queries.shape), grad_key.reshape(key_rows.shape), grad_value.reshape(key_rows.shape))

def spread_slots(slot_grads, slot_ids, window_count):
    slot_hits = (slot_ids[:, :, None] == jnp.arange(window_count, dtype=jnp.int32)[None, None, :]).astype(jnp.float32)
    blocks = slot_grads.reshape(slot_grads.shape[0], slot_ids.shape[0], slot_ids.shape[1], slot_grads.shape[2] // slot_ids.shape[1], slot_grads.shape[3])
    return jnp.einsum('njw,cnjmx->cwmx', slot_hits, blocks, precision=lax.Precision.HIGHEST)

def reference(video_query, video_key, video_value, audio_key, audio_value, cross_gate, out_cotangent, tile_list, tile_count, audio_list):
    gated_all = (cross_gate * out_cotangent).astype(jnp.bfloat16)
    video_padded = jnp.pad(jnp.stack((video_key, video_value)), ((0, 0), (0, 0), (TV_DEV, TV_DEV), (0, 0)))
    audio_padded = jnp.pad(jnp.stack((audio_key, audio_value)), ((0, 0), (0, 0), (TA_DEV, TA_DEV), (0, 0)))
    slot_order = jnp.arange(KB, dtype=jnp.int32)

    def one_window(state, position):
        video_grads, audio_grads, gate_total = state
        first_row = position * TV_DEV
        first_tile = position * TILES_DEV

        def rows_of(array):
            return lax.dynamic_slice_in_dim(array, first_row, TV_DEV, 1).reshape(CLIPS, TILES_DEV, TILE, DIM)
        queries = rows_of(video_query)
        cotangent = rows_of(out_cotangent)
        gated_rows = rows_of(gated_all)
        video_window = lax.dynamic_slice_in_dim(video_padded, first_row, 3 * TV_DEV, 2).reshape(2, CLIPS, 3 * TILES_DEV, TILE, DIM)
        audio_window = lax.dynamic_slice_in_dim(audio_padded, position * TA_DEV, 3 * TA_DEV, 2).reshape(2, CLIPS, 3, TA_DEV, DIM)
        own_list = lax.dynamic_slice_in_dim(tile_list, first_tile, TILES_DEV, 0)
        own_count = lax.dynamic_slice_in_dim(tile_count, first_tile, TILES_DEV, 0)
        own_audio = lax.dynamic_slice_in_dim(audio_list, first_tile, TILES_DEV, 0)
        tile_ids = (own_list - first_tile + TILES_DEV).astype(jnp.int32)
        tile_mask = jnp.repeat(slot_order[None, :] < own_count[:, None], TILE, axis=1)
        audio_ids = (own_audio - position + 1).astype(jnp.int32)
        audio_mask = jnp.ones((TILES_DEV, KA * TA_DEV), dtype=bool)
        key_rows = gather_slots(video_window[0], tile_ids)
        value_rows = gather_slots(video_window[1], tile_ids)
        audio_keys = gather_slots(audio_window[0], audio_ids)
        audio_values = gather_slots(audio_window[1], audio_ids)
        mixed_video, total_video = attend(queries, key_rows, value_rows, tile_mask)
        mixed_cross, total_cross = attend(queries, audio_keys, audio_values, audio_mask)
        delta_video = head_sums(cotangent, mixed_video)
        delta_cross = head_sums(gated_rows, mixed_cross)
        query_video, key_video, value_video = attend_back(queries, cotangent, key_rows, value_rows, tile_mask, total_video, delta_video)
        query_cross, key_cross, value_cross = attend_back(queries, gated_rows, audio_keys, audio_values, audio_mask, total_cross, delta_cross)
        window_video = jnp.stack((spread_slots(key_video, tile_ids, 3 * TILES_DEV), spread_slots(value_video, tile_ids, 3 * TILES_DEV))).reshape(2, CLIPS, 3 * TV_DEV, DIM)
        window_audio = jnp.stack((spread_slots(key_cross, audio_ids, 3), spread_slots(value_cross, audio_ids, 3))).reshape(2, CLIPS, 3 * TA_DEV, DIM)
        video_grads = lax.dynamic_update_slice_in_dim(video_grads, lax.dynamic_slice_in_dim(video_grads, first_row, 3 * TV_DEV, 2) + window_video, first_row, 2)
        audio_first = position * TA_DEV
        audio_grads = lax.dynamic_update_slice_in_dim(audio_grads, lax.dynamic_slice_in_dim(audio_grads, audio_first, 3 * TA_DEV, 2) + window_audio, audio_first, 2)
        gate_total = gate_total + lax.optimization_barrier(jnp.sum(cotangent.astype(jnp.float32) * mixed_cross, axis=(0, 1, 2)))
        query_rows = (query_video + query_cross).astype(jnp.bfloat16).reshape(CLIPS, TV_DEV, DIM)
        return ((video_grads, audio_grads, gate_total), query_rows)
    initial = (jnp.zeros(video_padded.shape, jnp.float32), jnp.zeros(audio_padded.shape, jnp.float32), jnp.zeros((DIM,), jnp.float32))
    final_state, query_rows = lax.scan(one_window, initial, jnp.arange(N_CTX, dtype=jnp.int32))
    video_grads, audio_grads, gate_total = final_state
    query_grad = jnp.transpose(query_rows, (1, 0, 2, 3)).reshape(CLIPS, TV, DIM)
    video_out = video_grads[:, :, TV_DEV:TV_DEV + TV].astype(jnp.bfloat16)
    audio_out = audio_grads[:, :, TA_DEV:TA_DEV + TA].astype(jnp.bfloat16)
    return (query_grad, video_out[0], video_out[1], audio_out[0], audio_out[1], gate_total)
```

```python
import functools
import math

import jax
import jax.numpy as jnp
from jax import lax
from jax.experimental import pallas as pl
from jax.experimental.pallas import tpu as pltpu
from jax.sharding import PartitionSpec as P

HEAD_DIM = 128
TILE = 64
SCALE = 1.0 / math.sqrt(HEAD_DIM)
SCORE_FACTOR = SCALE * math.log2(math.e)
NEG_INF = float("-inf")


def dot_t(a, b):
    return lax.dot_general(a, b, (((1,), (1,)), ((), ())), preferred_element_type=jnp.float32)


def dot(a, b):
    return lax.dot_general(a, b, (((1,), (0,)), ((), ())), preferred_element_type=jnp.float32)


def dot_lead(a, b):
    return lax.dot_general(a, b, (((0,), (0,)), ((), ())), preferred_element_type=jnp.float32)


def mate_of(position):
    return position + 1 - 2 * lax.rem(position, 2)


def far_of(position):
    return position - 1 + 2 * lax.rem(position, 2)


def tile_bias(list_ref, count_ref, row_tile, key_tile):
    tiles, slots = list_ref.shape
    row = jnp.clip(row_tile, 0, tiles - 1)
    inside = row == row_tile
    hit = jnp.bool_(False)
    for j in range(slots):
        hit = hit | ((list_ref[row, j] == key_tile) & (j < count_ref[row]))
    return jnp.where(hit & inside, 0.0, NEG_INF).astype(jnp.float32)


def block_bias(list_ref, row_tile, block):
    tiles, slots = list_ref.shape
    row = jnp.clip(row_tile, 0, tiles - 1)
    inside = row == row_tile
    hit = jnp.bool_(False)
    for j in range(slots):
        hit = hit | (list_ref[row, j] == block)
    return jnp.where(hit & inside, 0.0, NEG_INF).astype(jnp.float32)


def lanes_of(first, second):
    lane = lax.broadcasted_iota(jnp.int32, (1, 2 * TILE), 1)
    return jnp.where(lane < TILE, first, second)


def own_video_rows(list_ref, count_ref, position):
    rows = []
    for holder in (position, mate_of(position), far_of(position)):
        for w in range(2):
            key_tile = 2 * holder + w
            rows.append(
                lanes_of(
                    tile_bias(list_ref, count_ref, 2 * position, key_tile),
                    tile_bias(list_ref, count_ref, 2 * position + 1, key_tile),
                )
            )
    return rows


def own_audio_rows(list_ref, position):
    rows = []
    for block in (position, mate_of(position), far_of(position)):
        rows.append(
            lanes_of(
                block_bias(list_ref, 2 * position, block),
                block_bias(list_ref, 2 * position + 1, block),
            )
        )
    return rows


def masked(scores, rows, height):
    return jnp.concatenate(
        [scores[i * height : (i + 1) * height] * SCORE_FACTOR + row for i, row in enumerate(rows)],
        axis=0,
    )


def softmax_cols(scores):
    top = jnp.max(scores, axis=0, keepdims=True)
    grown = jnp.exp2(scores - top)
    total = jnp.sum(grown, axis=0, keepdims=True)
    return grown * (1.0 / total), top + jnp.log2(total)


def gate_kernel(position_ref, audio_list, q_ref, do_ref, ak0, ak1, ak2, av0, av1, av2, gate_out):
    rows = own_audio_rows(audio_list, position_ref[0])
    block = ak0.shape[0]
    for h in range(q_ref.shape[1] // HEAD_DIM):
        cols = slice(h * HEAD_DIM, (h + 1) * HEAD_DIM)
        keys = jnp.concatenate([ak0[:, cols], ak1[:, cols], ak2[:, cols]], axis=0)
        values = jnp.concatenate([av0[:, cols], av1[:, cols], av2[:, cols]], axis=0)
        scores = masked(dot_t(keys, q_ref[:, cols]), rows, block)
        prob, _ = softmax_cols(scores)
        spread = dot(prob.astype(jnp.bfloat16), do_ref[:, cols])
        gate_out[:, cols] = jnp.sum(spread * values.astype(jnp.float32), axis=0, keepdims=True)


def own_kernel(
    position_ref,
    tile_list,
    tile_count,
    audio_list,
    q_ref,
    do_ref,
    k0,
    k1,
    k2,
    v0,
    v1,
    v2,
    ak0,
    ak1,
    ak2,
    av0,
    av1,
    av2,
    gate_ref,
    dq_out,
    dk_out,
    dv_out,
    dak_out,
    dav_out,
    stat_out,
):
    position = position_ref[0]
    video_rows = own_video_rows(tile_list, tile_count, position)
    audio_rows = own_audio_rows(audio_list, position)
    own = k0.shape[0]
    window = 3 * own
    block = ak0.shape[0]
    for h in range(q_ref.shape[1] // HEAD_DIM):
        cols = slice(h * HEAD_DIM, (h + 1) * HEAD_DIM)
        q = q_ref[:, cols]
        do = do_ref[:, cols]
        gated = (gate_ref[:, cols] * do.astype(jnp.float32)).astype(jnp.bfloat16)
        keys = jnp.concatenate([r[:, cols] for r in (k0, k1, k2, ak0, ak1, ak2)], axis=0)
        raw = dot_t(keys, q)
        video_prob, video_total = softmax_cols(masked(raw[:window], video_rows, TILE))
        cross_prob, cross_total = softmax_cols(masked(raw[window:], audio_rows, block))
        video_weights = video_prob.astype(jnp.bfloat16)
        cross_weights = cross_prob.astype(jnp.bfloat16)
        values = jnp.concatenate([r[:, cols] for r in (v0, v1, v2)], axis=0)
        audio_values = jnp.concatenate([r[:, cols] for r in (av0, av1, av2)], axis=0)
        video_dp = dot_t(values, do)
        cross_dp = dot_t(audio_values, gated)
        video_delta = jnp.sum(video_weights.astype(jnp.float32) * video_dp, axis=0, keepdims=True)
        cross_delta = jnp.sum(cross_weights.astype(jnp.float32) * cross_dp, axis=0, keepdims=True)
        video_ds = (video_prob * (video_dp - video_delta)).astype(jnp.bfloat16)
        cross_ds = (cross_prob * (cross_dp - cross_delta)).astype(jnp.bfloat16)
        both_ds = jnp.concatenate([video_ds, cross_ds], axis=0)
        dq_out[:, cols] = (dot_lead(both_ds, keys) * SCALE).astype(jnp.bfloat16)
        dk_out[:, cols] = dot(video_ds[:own], q)
        dv_out[:, cols] = dot(video_weights[:own], do)
        dak_out[:, cols] = dot(cross_ds[:block], q)
        dav_out[:, cols] = dot(cross_weights[:block], gated)
        stat_out[4 * h : 4 * h + 4, :] = jnp.concatenate(
            [video_total, video_delta, cross_total, cross_delta], axis=0
        )


def beside_kernel(
    far,
    last,
    position_ref,
    tile_list,
    tile_count,
    audio_list,
    q_ref,
    do_ref,
    stat_ref,
    k_ref,
    v_ref,
    ak_ref,
    av_ref,
    gate_ref,
    dk_in,
    dv_in,
    dak_in,
    dav_in,
    dk_out,
    dv_out,
    dak_out,
    dav_out,
):
    position = position_ref[0]
    beside = far_of(position) if far else mate_of(position)
    video_rows = [
        lanes_of(
            tile_bias(tile_list, tile_count, 2 * beside, 2 * position + w),
            tile_bias(tile_list, tile_count, 2 * beside + 1, 2 * position + w),
        )
        for w in range(2)
    ]
    audio_row = lanes_of(
        block_bias(audio_list, 2 * beside, position),
        block_bias(audio_list, 2 * beside + 1, position),
    )
    own = k_ref.shape[0]
    factor = SCALE if last else 1.0
    for h in range(q_ref.shape[1] // HEAD_DIM):
        cols = slice(h * HEAD_DIM, (h + 1) * HEAD_DIM)
        q = q_ref[:, cols]
        do = do_ref[:, cols]
        gated = (gate_ref[:, cols] * do.astype(jnp.float32)).astype(jnp.bfloat16)
        stats = stat_ref[4 * h : 4 * h + 4, :]
        keys = jnp.concatenate([k_ref[:, cols], ak_ref[:, cols]], axis=0)
        raw = dot_t(keys, q)
        video_prob = jnp.exp2(masked(raw[:own], video_rows, TILE) - stats[0:1])
        cross_prob = jnp.exp2(raw[own:] * SCORE_FACTOR + audio_row - stats[2:3])
        video_dp = dot_t(v_ref[:, cols], do)
        cross_dp = dot_t(av_ref[:, cols], gated)
        video_ds = (video_prob * (video_dp - stats[1:2])).astype(jnp.bfloat16)
        cross_ds = (cross_prob * (cross_dp - stats[3:4])).astype(jnp.bfloat16)
        from_q = dot(jnp.concatenate([video_ds, cross_ds], axis=0), q)
        dk_out[:, cols] = ((dk_in[:, cols] + from_q[:own]) * factor).astype(dk_out.dtype)
        dak_out[:, cols] = ((dak_in[:, cols] + from_q[own:]) * factor).astype(dak_out.dtype)
        dv_out[:, cols] = (dv_in[:, cols] + dot(video_prob.astype(jnp.bfloat16), do)).astype(
            dv_out.dtype
        )
        dav_out[:, cols] = (dav_in[:, cols] + dot(cross_prob.astype(jnp.bfloat16), gated)).astype(
            dav_out.dtype
        )


def heads_per_step(heads, most):
    return max(g for g in range(1, most + 1) if heads % g == 0)


SMEM = pl.BlockSpec(memory_space=pltpu.SMEM)


def cols_spec(rows, width):
    return pl.BlockSpec((rows, width), lambda i: (0, i))


def cost(flops, arrays):
    return pl.CostEstimate(
        flops=flops,
        bytes_accessed=sum(a.size * a.dtype.itemsize for a in arrays),
        transcendentals=0,
    )


def per_device(
    video_query,
    video_key,
    video_value,
    audio_key,
    audio_value,
    cross_gate,
    out_cotangent,
    tile_list,
    tile_count,
    audio_list,
):
    clips, rows, width = video_query.shape
    block = audio_key.shape[1]
    heads = width // HEAD_DIM
    count = lax.axis_size("ctx")
    position = lax.axis_index("ctx").astype(jnp.int32).reshape(1)
    mate_pairs = [(i, i ^ 1) for i in range(count)]
    far_pairs = [(i + s, i + 1 - s) for i in range(1, count - 1, 2) for s in range(2)]

    def to_mate(x):
        return lax.ppermute(x, "ctx", mate_pairs)

    def to_far(x):
        return lax.ppermute(x, "ctx", far_pairs)

    q, k, v, do = (x.reshape(rows, width) for x in (video_query, video_key, video_value, out_cotangent))
    ak, av = (x.reshape(block, width) for x in (audio_key, audio_value))
    gate = cross_gate.reshape(1, width)

    ak_far, av_far = to_far(ak), to_far(av)
    ak_mate, av_mate = to_mate(ak), to_mate(av)
    k_far, v_far = to_far(k), to_far(v)
    k_mate, v_mate = to_mate(k), to_mate(v)
    q_far, do_far = to_far(q), to_far(do)
    q_mate, do_mate = to_mate(q), to_mate(do)

    group = heads_per_step(heads, 4)
    step = group * HEAD_DIM
    grid = (heads // group,)
    vspec = cols_spec(rows, step)
    aspec = cols_spec(block, step)
    gspec = cols_spec(1, step)
    sspec = pl.BlockSpec((4 * group, rows), lambda i: (i, 0))
    f32, bf16 = jnp.float32, jnp.bfloat16

    def array(n, dtype):
        return jax.ShapeDtypeStruct((n, width), dtype)

    gate_args = (q, do, ak, ak_mate, ak_far, av, av_mate, av_far)
    gate_part = pl.pallas_call(
        gate_kernel,
        grid=grid,
        in_specs=[SMEM, SMEM] + [vspec] * 2 + [aspec] * 6,
        out_specs=gspec,
        out_shape=array(1, f32),
        cost_estimate=cost(4 * rows * 3 * block * width, gate_args),
        name="gate_terms",
    )(position, audio_list, *gate_args)

    own_args = (q, do, k, k_mate, k_far, v, v_mate, v_far, ak, ak_mate, ak_far, av, av_mate, av_far)
    dq, dk, dv, dak, dav, stats = pl.pallas_call(
        own_kernel,
        grid=grid,
        in_specs=[SMEM] * 4 + [vspec] * 8 + [aspec] * 6 + [gspec],
        out_specs=[vspec] * 3 + [aspec] * 2 + [sspec],
        out_shape=[
            array(rows, bf16),
            array(rows, f32),
            array(rows, f32),
            array(block, f32),
            array(block, f32),
            jax.ShapeDtypeStruct((4 * heads, rows), f32),
        ],
        cost_estimate=cost(22 * rows * rows * width, own_args),
        name="own_queries",
    )(position, tile_list, tile_count, audio_list, *own_args, gate)

    stats_far, stats_mate = to_far(stats), to_mate(stats)

    def beside(far, last, q, do, stats, sums):
        out = bf16 if last else f32
        return pl.pallas_call(
            functools.partial(beside_kernel, far, last),
            grid=grid,
            in_specs=[SMEM] * 4
            + [vspec] * 2
            + [sspec]
            + [vspec] * 2
            + [aspec] * 2
            + [gspec]
            + [vspec] * 2
            + [aspec] * 2,
            out_specs=[vspec] * 2 + [aspec] * 2,
            out_shape=[array(rows, out), array(rows, out), array(block, out), array(block, out)],
            cost_estimate=cost(8 * rows * rows * width, (q, do, k, v) + tuple(sums)),
            name="far_queries" if far else "mate_queries",
        )(position, tile_list, tile_count, audio_list, q, do, stats, k, v, ak, av, gate, *sums)

    sums = beside(False, False, q_mate, do_mate, stats_mate, (dk, dv, dak, dav))
    dk, dv, dak, dav = beside(True, True, q_far, do_far, stats_far, sums)

    total = gate_part
    for axis in ("ctx", "dp"):
        size = lax.axis_size(axis)
        step_bit = 1
        while step_bit < size:
            total = total + lax.ppermute(total, axis, [(i, i ^ step_bit) for i in range(size)])
            step_bit *= 2

    return (
        dq.reshape(clips, rows, width),
        dk.reshape(clips, rows, width),
        dv.reshape(clips, rows, width),
        dak.reshape(clips, block, width),
        dav.reshape(clips, block, width),
        total.reshape(width),
    )


def solution(mesh):
    placed = P("dp", "ctx", None)
    return jax.shard_map(
        per_device,
        mesh=mesh,
        in_specs=(placed,) * 5 + (P(), placed, P(), P(), P()),
        out_specs=(placed,) * 5 + (P(),),
        check_vma=False,
    )
```

```python
import math

import jax
import jax.numpy as jnp
from jax import lax
from jax.experimental import pallas as pl
from jax.experimental.pallas import tpu as pltpu
from jax.sharding import PartitionSpec as P

HEAD_DIM = 128
TILE = 64
SCALE = 1.0 / math.sqrt(HEAD_DIM)
SCORE_FACTOR = SCALE * math.log2(math.e)
NEG_INF = float("-inf")


def dot_t(a, b):
    return lax.dot_general(a, b, (((1,), (1,)), ((), ())), preferred_element_type=jnp.float32)


def dot(a, b):
    return lax.dot_general(a, b, (((1,), (0,)), ((), ())), preferred_element_type=jnp.float32)


def dot_lead(a, b):
    return lax.dot_general(a, b, (((0,), (0,)), ((), ())), preferred_element_type=jnp.float32)


def mate_of(position):
    return position + 1 - 2 * lax.rem(position, 2)


def far_of(position):
    return position - 1 + 2 * lax.rem(position, 2)


def tile_bias(list_ref, count_ref, row_tile, key_tile):
    slots, tiles = list_ref.shape
    row = jnp.clip(row_tile, 0, tiles - 1)
    inside = row == row_tile
    hit = jnp.bool_(False)
    for j in range(slots):
        hit = hit | ((list_ref[j, row] == key_tile) & (j < count_ref[row]))
    return jnp.where(hit & inside, 0.0, NEG_INF).astype(jnp.float32)


def block_bias(list_ref, row_tile, block):
    slots, tiles = list_ref.shape
    row = jnp.clip(row_tile, 0, tiles - 1)
    inside = row == row_tile
    hit = jnp.bool_(False)
    for j in range(slots):
        hit = hit | (list_ref[j, row] == block)
    return jnp.where(hit & inside, 0.0, NEG_INF).astype(jnp.float32)


def lanes_of(first, second):
    lane = lax.broadcasted_iota(jnp.int32, (1, 2 * TILE), 1)
    return jnp.where(lane < TILE, first, second)


def own_video_rows(list_ref, count_ref, position):
    rows = []
    for holder in (position, mate_of(position), far_of(position)):
        for w in range(2):
            key_tile = 2 * holder + w
            rows.append(
                lanes_of(
                    tile_bias(list_ref, count_ref, 2 * position, key_tile),
                    tile_bias(list_ref, count_ref, 2 * position + 1, key_tile),
                )
            )
    return rows


def own_audio_rows(list_ref, position):
    rows = []
    for block in (position, mate_of(position), far_of(position)):
        rows.append(
            lanes_of(
                block_bias(list_ref, 2 * position, block),
                block_bias(list_ref, 2 * position + 1, block),
            )
        )
    return rows


def masked(scores, rows, height):
    return jnp.concatenate(
        [scores[i * height : (i + 1) * height] * SCORE_FACTOR + row for i, row in enumerate(rows)],
        axis=0,
    )


def softmax_cols(scores):
    top = jnp.max(scores, axis=0, keepdims=True)
    grown = jnp.exp2(scores - top)
    total = jnp.sum(grown, axis=0, keepdims=True)
    return grown * (1.0 / total), top + jnp.log2(total)


def head_cols(ref):
    return [slice(i, i + HEAD_DIM) for i in range(0, ref.shape[1], HEAD_DIM)]


def rows_at(refs, first, count, cols):
    return jnp.concatenate([ref[first : first + count, cols] for ref in refs], axis=0)


def gated_by(gate, cotangent):
    return (gate * cotangent.astype(jnp.float32)).astype(jnp.bfloat16)


def gate_kernel(position_ref, audio_list, q_ref, do_ref, a0, a1, a2, gate_out):
    rows = own_audio_rows(audio_list, position_ref[0])
    block = a0.shape[0] // 2
    heads = head_cols(q_ref)
    raw = [dot_t(rows_at((a0, a1, a2), 0, block, c), q_ref[:, c]) for c in heads]
    weights = [softmax_cols(masked(r, rows, block))[0].astype(jnp.bfloat16) for r in raw]
    spread = [dot(w, do_ref[:, c]) for w, c in zip(weights, heads)]
    for t, c in zip(spread, heads):
        values = rows_at((a0, a1, a2), block, block, c).astype(jnp.float32)
        gate_out[:, c] = jnp.sum(t * values, axis=0, keepdims=True)


def own_kernel(
    position_ref,
    tile_list,
    tile_count,
    audio_list,
    q_ref,
    do_ref,
    kv0,
    kv1,
    kv2,
    a0,
    a1,
    a2,
    gate_ref,
    dq_out,
    own_out,
    mate_k_out,
    mate_v_out,
    stat_out,
):
    position = position_ref[0]
    video_rows = own_video_rows(tile_list, tile_count, position)
    audio_rows = own_audio_rows(audio_list, position)
    own = kv0.shape[0] // 2
    window = 3 * own
    block = a0.shape[0] // 2
    video, audio = (kv0, kv1, kv2), (a0, a1, a2)
    heads = head_cols(q_ref)
    products = []
    for c in heads:
        q = q_ref[:, c]
        do = do_ref[:, c]
        keys = jnp.concatenate([rows_at(video, 0, own, c), rows_at(audio, 0, block, c)], axis=0)
        raw = dot_t(keys, q)
        video_dp = dot_t(rows_at(video, own, own, c), do)
        cross_dp = dot_t(rows_at(audio, block, block, c), gated_by(gate_ref[:, c], do))
        products.append((raw, video_dp, cross_dp))
    grads = []
    for h, (raw, video_dp, cross_dp) in enumerate(products):
        video_prob, video_total = softmax_cols(masked(raw[:window], video_rows, TILE))
        cross_prob, cross_total = softmax_cols(masked(raw[window:], audio_rows, block))
        video_weights = video_prob.astype(jnp.bfloat16)
        cross_weights = cross_prob.astype(jnp.bfloat16)
        video_delta = jnp.sum(video_weights.astype(jnp.float32) * video_dp, axis=0, keepdims=True)
        cross_delta = jnp.sum(cross_weights.astype(jnp.float32) * cross_dp, axis=0, keepdims=True)
        video_ds = (video_prob * (video_dp - video_delta)).astype(jnp.bfloat16)
        cross_ds = (cross_prob * (cross_dp - cross_delta)).astype(jnp.bfloat16)
        stat_out[4 * h : 4 * h + 4, :] = jnp.concatenate(
            [video_total, video_delta, cross_total, cross_delta], axis=0
        )
        grads.append((video_ds, cross_ds, video_weights[: 2 * own], cross_weights[: 2 * block]))
    for c, (video_ds, cross_ds, video_weights, cross_weights) in zip(heads, grads):
        q = q_ref[:, c]
        do = do_ref[:, c]
        keys = jnp.concatenate([rows_at(video, 0, own, c), rows_at(audio, 0, block, c)], axis=0)
        both_ds = jnp.concatenate([video_ds, cross_ds], axis=0)
        dq_out[:, c] = (dot_lead(both_ds, keys) * SCALE).astype(jnp.bfloat16)
        dk = dot(video_ds[: 2 * own], q)
        dv = dot(video_weights, do)
        dak = dot(cross_ds[: 2 * block], q)
        dav = dot(cross_weights, gated_by(gate_ref[:, c], do))
        own_out[:own, c] = dk[:own]
        own_out[own : 2 * own, c] = dv[:own]
        own_out[2 * own : 2 * own + block, c] = dak[:block]
        own_out[2 * own + block :, c] = dav[:block]
        mate_k_out[:own, c] = dk[own:].astype(jnp.bfloat16)
        mate_k_out[own:, c] = dak[block:].astype(jnp.bfloat16)
        mate_v_out[:own, c] = dv[own:].astype(jnp.bfloat16)
        mate_v_out[own:, c] = dav[block:].astype(jnp.bfloat16)


def far_kernel(
    position_ref,
    tile_list,
    tile_count,
    audio_list,
    qo_ref,
    stat_ref,
    kv_ref,
    a_ref,
    gate_ref,
    own_in,
    mate_k_in,
    mate_v_in,
    dk_out,
    dv_out,
    dak_out,
    dav_out,
):
    position = position_ref[0]
    beside = far_of(position)
    video_rows = [
        lanes_of(
            tile_bias(tile_list, tile_count, 2 * beside, 2 * position + w),
            tile_bias(tile_list, tile_count, 2 * beside + 1, 2 * position + w),
        )
        for w in range(2)
    ]
    audio_row = lanes_of(
        block_bias(audio_list, 2 * beside, position),
        block_bias(audio_list, 2 * beside + 1, position),
    )
    own = kv_ref.shape[0] // 2
    block = a_ref.shape[0] // 2
    heads = head_cols(kv_ref)
    products = []
    for c in heads:
        q = qo_ref[:own, c]
        do = qo_ref[own:, c]
        keys = jnp.concatenate([kv_ref[:own, c], a_ref[:block, c]], axis=0)
        products.append(
            (
                dot_t(keys, q),
                dot_t(kv_ref[own:, c], do),
                dot_t(a_ref[block:, c], gated_by(gate_ref[:, c], do)),
            )
        )
    grads = []
    for h, (raw, video_dp, cross_dp) in enumerate(products):
        stats = stat_ref[4 * h : 4 * h + 4, :]
        video_prob = jnp.exp2(masked(raw[:own], video_rows, TILE) - stats[0:1])
        cross_prob = jnp.exp2(raw[own:] * SCORE_FACTOR + audio_row - stats[2:3])
        video_ds = (video_prob * (video_dp - stats[1:2])).astype(jnp.bfloat16)
        cross_ds = (cross_prob * (cross_dp - stats[3:4])).astype(jnp.bfloat16)
        grads.append(
            (
                jnp.concatenate([video_ds, cross_ds], axis=0),
                video_prob.astype(jnp.bfloat16),
                cross_prob.astype(jnp.bfloat16),
            )
        )
    for c, (both_ds, video_weights, cross_weights) in zip(heads, grads):
        q = qo_ref[:own, c]
        do = qo_ref[own:, c]
        from_q = dot(both_ds, q)
        from_do = dot(video_weights, do)
        from_gated = dot(cross_weights, gated_by(gate_ref[:, c], do))
        mate_k = mate_k_in[:, c].astype(jnp.float32)
        mate_v = mate_v_in[:, c].astype(jnp.float32)
        sums = own_in[:, c]
        audio = sums[2 * own :]
        dk_out[:, c] = ((sums[:own] + mate_k[:own] + from_q[:own]) * SCALE).astype(dk_out.dtype)
        dv_out[:, c] = (sums[own : 2 * own] + mate_v[:own] + from_do).astype(dv_out.dtype)
        dak_out[:, c] = ((audio[:block] + mate_k[own:] + from_q[own:]) * SCALE).astype(dak_out.dtype)
        dav_out[:, c] = (audio[block:] + mate_v[own:] + from_gated).astype(dav_out.dtype)


def heads_per_step(heads, most):
    return max(g for g in range(1, most + 1) if heads % g == 0)


def flipped(part, axis, bit):
    size = lax.axis_size(axis)
    flips = [f for f in (bit, 2 * bit, 3 * bit) if f < size]
    return [part] + [lax.ppermute(part, axis, [(i, i ^ f) for i in range(size)]) for f in flips]


def joined(parts):
    if len(parts) < 4:
        return sum(parts[1:], parts[0])
    return (parts[0] + parts[1]) + (parts[2] + parts[3])


def after(first, then):
    return lax.optimization_barrier((first, then))


SMEM = pl.BlockSpec(memory_space=pltpu.SMEM)


def cols_spec(rows, width):
    return pl.BlockSpec((rows, width), lambda i: (0, i))


def cost(flops, arrays):
    return pl.CostEstimate(
        flops=flops,
        bytes_accessed=0,
        transcendentals=0,
    )


def per_device(
    video_query,
    video_key,
    video_value,
    audio_key,
    audio_value,
    cross_gate,
    out_cotangent,
    tile_list,
    tile_count,
    audio_list,
):
    clips, rows, width = video_query.shape
    block = audio_key.shape[1]
    heads = width // HEAD_DIM
    count = lax.axis_size("ctx")
    position = lax.axis_index("ctx").astype(jnp.int32).reshape(1)
    mate_pairs = [(i, i ^ 1) for i in range(count)]
    far_pairs = [(i + s, i + 1 - s) for i in range(1, count - 1, 2) for s in range(2)]

    def to_mate(x):
        return lax.ppermute(x, "ctx", mate_pairs)

    def to_far(x):
        return lax.ppermute(x, "ctx", far_pairs)

    q, k, v, do = (x.reshape(rows, width) for x in (video_query, video_key, video_value, out_cotangent))
    ak, av = (x.reshape(block, width) for x in (audio_key, audio_value))
    gate = cross_gate.reshape(1, width)
    tile_list, audio_list = tile_list.T, audio_list.T

    a = jnp.concatenate([ak, av], axis=0)
    a_far, a_mate = to_far(a), to_mate(a)
    kv = jnp.concatenate([k, v], axis=0)
    kv_far, kv_mate = to_far(kv), to_mate(kv)

    f32, bf16 = jnp.float32, jnp.bfloat16

    def specs(group):
        step = group * HEAD_DIM
        return (
            (heads // group,),
            cols_spec(2 * rows, step),
            cols_spec(rows, step),
            cols_spec(2 * block, step),
            cols_spec(block, step),
            cols_spec(1, step),
            pl.BlockSpec((4 * group, rows), lambda i: (i, 0)),
        )

    def array(n, dtype):
        return jax.ShapeDtypeStruct((n, width), dtype)

    params = pltpu.CompilerParams(vmem_limit_bytes=24 * 2**20)

    grid, pair, vspec, apair, aspec, gspec, sspec = specs(heads_per_step(heads, 12))
    gate_args = (q, do, a, a_mate, a_far)
    gate_part = pl.pallas_call(
        gate_kernel,
        grid=grid,
        in_specs=[SMEM, SMEM] + [vspec] * 2 + [apair] * 3,
        out_specs=gspec,
        out_shape=array(1, f32),
        cost_estimate=cost(20_000_000_000, gate_args),
        compiler_params=params,
        name="gate_terms",
    )(position, audio_list, *gate_args)

    total = joined(flipped(gate_part, "dp", 1))
    parts = flipped(total, "ctx", 16)
    kv_far, parts = after(kv_far, parts)
    total, q_next = after(joined(parts), q)
    qo_far = to_far(jnp.concatenate([q_next, do], axis=0))

    grid, pair, vspec, apair, aspec, gspec, sspec = specs(heads_per_step(heads, 8))
    sums_spec = cols_spec(2 * (rows + block), vspec.block_shape[1])
    half_spec = cols_spec(rows + block, vspec.block_shape[1])
    own_args = (q, do, kv, kv_mate, kv_far, a, a_mate, a_far)
    dq, own_sums, mate_k, mate_v, stats = pl.pallas_call(
        own_kernel,
        grid=grid,
        in_specs=[SMEM] * 4 + [vspec] * 2 + [pair] * 3 + [apair] * 3 + [gspec],
        out_specs=[vspec, sums_spec, half_spec, half_spec, sspec],
        out_shape=[
            array(rows, bf16),
            array(2 * (rows + block), f32),
            array(rows + block, bf16),
            array(rows + block, bf16),
            jax.ShapeDtypeStruct((4 * heads, rows), f32),
        ],
        cost_estimate=cost(0, own_args),
        compiler_params=params,
        name="own_queries",
    )(position, tile_list, tile_count, audio_list, *own_args, gate)

    stats_far = to_far(stats)
    mate_k, mate_v = to_mate(mate_k), to_mate(mate_v)
    (mate_k, mate_v), total = after((mate_k, mate_v), total)
    parts = flipped(total, "ctx", 1)
    (qo_far, stats_far), parts = after((qo_far, stats_far), parts)
    total = joined(flipped(joined(parts), "ctx", 4))

    far_args = (qo_far, stats_far, kv, a, gate, own_sums, mate_k, mate_v)
    dk, dv, dak, dav = pl.pallas_call(
        far_kernel,
        grid=grid,
        in_specs=[SMEM] * 4 + [pair, sspec, pair, apair, gspec, sums_spec, half_spec, half_spec],
        out_specs=[vspec, vspec, aspec, aspec],
        out_shape=[array(rows, bf16), array(rows, bf16), array(block, bf16), array(block, bf16)],
        cost_estimate=cost(5_000_000_000, far_args),
        compiler_params=params,
        name="far_queries",
    )(position, tile_list, tile_count, audio_list, *far_args)

    return (
        dq.reshape(clips, rows, width),
        dk.reshape(clips, rows, width),
        dv.reshape(clips, rows, width),
        dak.reshape(clips, block, width),
        dav.reshape(clips, block, width),
        total.reshape(width),
    )


def solution(mesh):
    placed = P("dp", "ctx", None)
    return jax.shard_map(
        per_device,
        mesh=mesh,
        in_specs=(placed,) * 5 + (P(), placed, P(), P(), P()),
        out_specs=(placed,) * 5 + (P(),),
        check_vma=False,
    )
```

```python
import math

import jax
import jax.numpy as jnp
from jax import lax
from jax.experimental import pallas as pl
from jax.experimental.pallas import tpu as pltpu
from jax.sharding import PartitionSpec as P

HEAD_DIM = 128
TILE = 64
SCALE = 1.0 / math.sqrt(HEAD_DIM)
SCORE_FACTOR = SCALE * math.log2(math.e)
NEG_INF = float("-inf")


def dot_t(a, b):
    return lax.dot_general(a, b, (((1,), (1,)), ((), ())), preferred_element_type=jnp.float32)


def dot(a, b):
    return lax.dot_general(a, b, (((1,), (0,)), ((), ())), preferred_element_type=jnp.float32)


def dot_lead(a, b):
    return lax.dot_general(a, b, (((0,), (0,)), ((), ())), preferred_element_type=jnp.float32)


def mate_of(position):
    return position + 1 - 2 * lax.rem(position, 2)


def far_of(position):
    return position - 1 + 2 * lax.rem(position, 2)


def tile_bias(list_ref, count_ref, row_tile, key_tile):
    slots, tiles = list_ref.shape
    row = jnp.clip(row_tile, 0, tiles - 1)
    inside = row == row_tile
    hit = jnp.bool_(False)
    for j in range(slots):
        hit = hit | ((list_ref[j, row] == key_tile) & (j < count_ref[row]))
    return jnp.where(hit & inside, 0.0, NEG_INF).astype(jnp.float32)


def block_bias(list_ref, row_tile, block):
    slots, tiles = list_ref.shape
    row = jnp.clip(row_tile, 0, tiles - 1)
    inside = row == row_tile
    hit = jnp.bool_(False)
    for j in range(slots):
        hit = hit | (list_ref[j, row] == block)
    return jnp.where(hit & inside, 0.0, NEG_INF).astype(jnp.float32)


def lanes_of(first, second):
    lane = lax.broadcasted_iota(jnp.int32, (1, 2 * TILE), 1)
    return jnp.where(lane < TILE, first, second)


def own_video_rows(list_ref, count_ref, position):
    rows = []
    for holder in (position, mate_of(position), far_of(position)):
        for w in range(2):
            key_tile = 2 * holder + w
            rows.append(
                lanes_of(
                    tile_bias(list_ref, count_ref, 2 * position, key_tile),
                    tile_bias(list_ref, count_ref, 2 * position + 1, key_tile),
                )
            )
    return rows


def own_audio_rows(list_ref, position):
    rows = []
    for block in (position, mate_of(position), far_of(position)):
        rows.append(
            lanes_of(
                block_bias(list_ref, 2 * position, block),
                block_bias(list_ref, 2 * position + 1, block),
            )
        )
    return rows


def masked(scores, rows, height):
    return jnp.concatenate(
        [scores[i * height : (i + 1) * height] * SCORE_FACTOR + row for i, row in enumerate(rows)],
        axis=0,
    )


def softmax_cols(scores):
    top = jnp.max(scores, axis=0, keepdims=True)
    grown = jnp.exp2(scores - top)
    total = jnp.sum(grown, axis=0, keepdims=True)
    return grown * (1.0 / total), top + jnp.log2(total)


def head_cols(ref):
    return [slice(i, i + HEAD_DIM) for i in range(0, ref.shape[1], HEAD_DIM)]


def rows_at(refs, first, count, cols):
    return jnp.concatenate([ref[first : first + count, cols] for ref in refs], axis=0)


def gated_by(gate, cotangent):
    return (gate * cotangent.astype(jnp.float32)).astype(jnp.bfloat16)


def gate_kernel(position_ref, audio_list, q_ref, do_ref, a0, a1, a2, gate_out):
    rows = own_audio_rows(audio_list, position_ref[0])
    block = a0.shape[0] // 2
    heads = head_cols(q_ref)
    raw = [dot_t(rows_at((a0, a1, a2), 0, block, c), q_ref[:, c]) for c in heads]
    weights = [softmax_cols(masked(r, rows, block))[0].astype(jnp.bfloat16) for r in raw]
    spread = [dot(w, do_ref[:, c]) for w, c in zip(weights, heads)]
    for t, c in zip(spread, heads):
        values = rows_at((a0, a1, a2), block, block, c).astype(jnp.float32)
        gate_out[:, c] = jnp.sum(t * values, axis=0, keepdims=True)


def own_kernel(
    position_ref,
    tile_list,
    tile_count,
    audio_list,
    q_ref,
    do_ref,
    kv0,
    kv1,
    kv2,
    a0,
    a1,
    a2,
    gate_ref,
    dq_out,
    own_out,
    mate_k_out,
    mate_v_out,
    stat_out,
):
    position = position_ref[0]
    video_rows = own_video_rows(tile_list, tile_count, position)
    audio_rows = own_audio_rows(audio_list, position)
    own = kv0.shape[0] // 2
    window = 3 * own
    block = a0.shape[0] // 2
    video, audio = (kv0, kv1, kv2), (a0, a1, a2)
    heads = head_cols(q_ref)
    products = []
    for c in heads:
        q = q_ref[:, c]
        do = do_ref[:, c]
        keys = jnp.concatenate([rows_at(video, 0, own, c), rows_at(audio, 0, block, c)], axis=0)
        raw = dot_t(keys, q)
        video_dp = dot_t(rows_at(video, own, own, c), do)
        cross_dp = dot_t(rows_at(audio, block, block, c), gated_by(gate_ref[:, c], do))
        products.append((raw, video_dp, cross_dp))
    grads = []
    for h, (raw, video_dp, cross_dp) in enumerate(products):
        video_prob, video_total = softmax_cols(masked(raw[:window], video_rows, TILE))
        cross_prob, cross_total = softmax_cols(masked(raw[window:], audio_rows, block))
        video_weights = video_prob.astype(jnp.bfloat16)
        cross_weights = cross_prob.astype(jnp.bfloat16)
        video_delta = jnp.sum(video_weights.astype(jnp.float32) * video_dp, axis=0, keepdims=True)
        cross_delta = jnp.sum(cross_weights.astype(jnp.float32) * cross_dp, axis=0, keepdims=True)
        video_ds = (video_prob * (video_dp - video_delta)).astype(jnp.bfloat16)
        cross_ds = (cross_prob * (cross_dp - cross_delta)).astype(jnp.bfloat16)
        stat_out[4 * h : 4 * h + 4, :] = jnp.concatenate(
            [video_total, video_delta, cross_total, cross_delta], axis=0
        )
        grads.append((video_ds, cross_ds, video_weights[: 2 * own], cross_weights[: 2 * block]))
    for c, (video_ds, cross_ds, video_weights, cross_weights) in zip(heads, grads):
        q = q_ref[:, c]
        do = do_ref[:, c]
        keys = jnp.concatenate([rows_at(video, 0, own, c), rows_at(audio, 0, block, c)], axis=0)
        both_ds = jnp.concatenate([video_ds, cross_ds], axis=0)
        dq_out[:, c] = (dot_lead(both_ds, keys) * SCALE).astype(jnp.bfloat16)
        dk = dot(video_ds[: 2 * own], q)
        dv = dot(video_weights, do)
        dak = dot(cross_ds[: 2 * block], q)
        dav = dot(cross_weights, gated_by(gate_ref[:, c], do))
        own_out[:own, c] = dk[:own]
        own_out[own : 2 * own, c] = dv[:own]
        own_out[2 * own : 2 * own + block, c] = dak[:block]
        own_out[2 * own + block :, c] = dav[:block]
        mate_k_out[:own, c] = dk[own:].astype(jnp.bfloat16)
        mate_k_out[own:, c] = dak[block:].astype(jnp.bfloat16)
        mate_v_out[:own, c] = dv[own:].astype(jnp.bfloat16)
        mate_v_out[own:, c] = dav[block:].astype(jnp.bfloat16)


def far_kernel(
    position_ref,
    tile_list,
    tile_count,
    audio_list,
    qo_ref,
    stat_ref,
    kv_ref,
    a_ref,
    gate_ref,
    own_in,
    mate_k_in,
    mate_v_in,
    dk_out,
    dv_out,
    dak_out,
    dav_out,
):
    position = position_ref[0]
    beside = far_of(position)
    video_rows = [
        lanes_of(
            tile_bias(tile_list, tile_count, 2 * beside, 2 * position + w),
            tile_bias(tile_list, tile_count, 2 * beside + 1, 2 * position + w),
        )
        for w in range(2)
    ]
    audio_row = lanes_of(
        block_bias(audio_list, 2 * beside, position),
        block_bias(audio_list, 2 * beside + 1, position),
    )
    own = kv_ref.shape[0] // 2
    block = a_ref.shape[0] // 2
    heads = head_cols(kv_ref)
    products = []
    for c in heads:
        q = qo_ref[:own, c]
        do = qo_ref[own:, c]
        keys = jnp.concatenate([kv_ref[:own, c], a_ref[:block, c]], axis=0)
        products.append(
            (
                dot_t(keys, q),
                dot_t(kv_ref[own:, c], do),
                dot_t(a_ref[block:, c], gated_by(gate_ref[:, c], do)),
            )
        )
    grads = []
    for h, (raw, video_dp, cross_dp) in enumerate(products):
        stats = stat_ref[4 * h : 4 * h + 4, :]
        video_prob = jnp.exp2(masked(raw[:own], video_rows, TILE) - stats[0:1])
        cross_prob = jnp.exp2(raw[own:] * SCORE_FACTOR + audio_row - stats[2:3])
        video_ds = (video_prob * (video_dp - stats[1:2])).astype(jnp.bfloat16)
        cross_ds = (cross_prob * (cross_dp - stats[3:4])).astype(jnp.bfloat16)
        grads.append(
            (
                jnp.concatenate([video_ds, cross_ds], axis=0),
                video_prob.astype(jnp.bfloat16),
                cross_prob.astype(jnp.bfloat16),
            )
        )
    for c, (both_ds, video_weights, cross_weights) in zip(heads, grads):
        q = qo_ref[:own, c]
        do = qo_ref[own:, c]
        from_q = dot(both_ds, q)
        from_do = dot(video_weights, do)
        from_gated = dot(cross_weights, gated_by(gate_ref[:, c], do))
        mate_k = mate_k_in[:, c].astype(jnp.float32)
        mate_v = mate_v_in[:, c].astype(jnp.float32)
        sums = own_in[:, c]
        audio = sums[2 * own :]
        dk_out[:, c] = ((sums[:own] + mate_k[:own] + from_q[:own]) * SCALE).astype(dk_out.dtype)
        dv_out[:, c] = (sums[own : 2 * own] + mate_v[:own] + from_do).astype(dv_out.dtype)
        dak_out[:, c] = ((audio[:block] + mate_k[own:] + from_q[own:]) * SCALE).astype(dak_out.dtype)
        dav_out[:, c] = (audio[block:] + mate_v[own:] + from_gated).astype(dav_out.dtype)


def heads_per_step(heads, most):
    return max(g for g in range(1, most + 1) if heads % g == 0)


def flipped(part, axis, bit, bits=2):
    size = lax.axis_size(axis)
    flips = [f * bit for f in range(1, 2**bits) if f * bit < size]
    return [part] + [lax.ppermute(part, axis, [(i, i ^ f) for i in range(size)]) for f in flips]


def flipped_apart(part):
    size = lax.axis_size("ctx")
    return [
        lax.ppermute(part, "ctx", [(i, i ^ (step + 8 * (i % 2))) for i in range(size)])
        for step in (0, 2, 4, 6)
    ]


def joined(parts):
    if len(parts) < 4:
        return sum(parts[1:], parts[0])
    return (parts[0] + parts[1]) + (parts[2] + parts[3])


def after(first, then):
    return lax.optimization_barrier((first, then))


SMEM = pl.BlockSpec(memory_space=pltpu.SMEM)


def cols_spec(rows, width):
    return pl.BlockSpec((rows, width), lambda i: (0, i))


def cost(flops, arrays):
    return pl.CostEstimate(
        flops=flops,
        bytes_accessed=0,
        transcendentals=0,
    )


def per_device(
    video_query,
    video_key,
    video_value,
    audio_key,
    audio_value,
    cross_gate,
    out_cotangent,
    tile_list,
    tile_count,
    audio_list,
):
    clips, rows, width = video_query.shape
    block = audio_key.shape[1]
    heads = width // HEAD_DIM
    count = lax.axis_size("ctx")
    position = lax.axis_index("ctx").astype(jnp.int32).reshape(1)
    mate_pairs = [(i, i ^ 1) for i in range(count)]
    far_pairs = [(i + s, i + 1 - s) for i in range(1, count - 1, 2) for s in range(2)]

    def to_mate(x):
        return lax.ppermute(x, "ctx", mate_pairs)

    def to_far(x):
        return lax.ppermute(x, "ctx", far_pairs)

    q, k, v, do = (x.reshape(rows, width) for x in (video_query, video_key, video_value, out_cotangent))
    ak, av = (x.reshape(block, width) for x in (audio_key, audio_value))
    gate = cross_gate.reshape(1, width)
    tile_list, audio_list = tile_list.T, audio_list.T

    a = jnp.concatenate([ak, av], axis=0)
    kv = jnp.concatenate([k, v], axis=0)
    kv, a = after(kv, a)
    a_far, a_mate = to_far(a), to_mate(a)
    kv_far, kv_mate = to_far(kv), to_mate(kv)

    f32, bf16 = jnp.float32, jnp.bfloat16

    def specs(group):
        step = group * HEAD_DIM
        return (
            (heads // group,),
            cols_spec(2 * rows, step),
            cols_spec(rows, step),
            cols_spec(2 * block, step),
            cols_spec(block, step),
            cols_spec(1, step),
            pl.BlockSpec((4 * group, rows), lambda i: (i, 0)),
        )

    def array(n, dtype):
        return jax.ShapeDtypeStruct((n, width), dtype)

    params = pltpu.CompilerParams(vmem_limit_bytes=24 * 2**20)

    grid, pair, vspec, apair, aspec, gspec, sspec = specs(heads_per_step(heads, 12))
    gate_args = (q, do, a, a_mate, a_far)
    gate_part = pl.pallas_call(
        gate_kernel,
        grid=grid,
        in_specs=[SMEM, SMEM] + [vspec] * 2 + [apair] * 3,
        out_specs=gspec,
        out_shape=array(1, f32),
        cost_estimate=cost(20_000_000_000, gate_args),
        compiler_params=params,
        name="gate_terms",
    )(position, audio_list, *gate_args)

    total = joined(flipped(joined(flipped(gate_part, "ctx", 1, 1)), "dp", 1))
    kv_mate, total = after(kv_mate, total)
    parts = flipped_apart(total)
    (kv_far, total), q_next = after((kv_far, total), q)
    kv_far, parts = after(kv_far, parts)
    total = joined(flipped(joined(parts), "ctx", 1, 1))
    qo_far = to_far(jnp.concatenate([q_next, do], axis=0))

    grid, pair, vspec, apair, aspec, gspec, sspec = specs(heads_per_step(heads, 8))
    sums_spec = cols_spec(2 * (rows + block), vspec.block_shape[1])
    half_spec = cols_spec(rows + block, vspec.block_shape[1])
    own_args = (q, do, kv, kv_mate, kv_far, a, a_mate, a_far)
    dq, own_sums, mate_k, mate_v, stats = pl.pallas_call(
        own_kernel,
        grid=grid,
        in_specs=[SMEM] * 4 + [vspec] * 2 + [pair] * 3 + [apair] * 3 + [gspec],
        out_specs=[vspec, sums_spec, half_spec, half_spec, sspec],
        out_shape=[
            array(rows, bf16),
            array(2 * (rows + block), f32),
            array(rows + block, bf16),
            array(rows + block, bf16),
            jax.ShapeDtypeStruct((4 * heads, rows), f32),
        ],
        cost_estimate=cost(20_000_000_000, own_args),
        compiler_params=params,
        name="own_queries",
    )(position, tile_list, tile_count, audio_list, *own_args, gate)

    stats_far = to_far(stats)
    mate_k, mate_v = to_mate(mate_k), to_mate(mate_v)
    (mate_k, mate_v), total = after((mate_k, mate_v), total)
    parts = flipped(total, "ctx", 16)

    far_args = (qo_far, stats_far, kv, a, gate, own_sums, mate_k, mate_v)
    dk, dv, dak, dav = pl.pallas_call(
        far_kernel,
        grid=grid,
        in_specs=[SMEM] * 4 + [pair, sspec, pair, apair, gspec, sums_spec, half_spec, half_spec],
        out_specs=[vspec, vspec, aspec, aspec],
        out_shape=[array(rows, bf16), array(rows, bf16), array(block, bf16), array(block, bf16)],
        cost_estimate=cost(5_000_000_000, far_args),
        compiler_params=params,
        name="far_queries",
    )(position, tile_list, tile_count, audio_list, *far_args)

    dak, parts = after(dak, parts)
    total = joined(parts)

    return (
        dq.reshape(clips, rows, width),
        dk.reshape(clips, rows, width),
        dv.reshape(clips, rows, width),
        dak.reshape(clips, block, width),
        dav.reshape(clips, block, width),
        total.reshape(width),
    )


def solution(mesh):
    placed = P("dp", "ctx", None)
    return jax.shard_map(
        per_device,
        mesh=mesh,
        in_specs=(placed,) * 5 + (P(), placed, P(), P(), P()),
        out_specs=(placed,) * 5 + (P(),),
        check_vma=False,
    )
```

```python
import math

import jax
import jax.numpy as jnp
from jax import lax
from jax.experimental import pallas as pl
from jax.experimental.pallas import tpu as pltpu
from jax.sharding import PartitionSpec as P

HEAD_DIM = 128
TILE = 64
SCALE = 1.0 / math.sqrt(HEAD_DIM)
SCORE_FACTOR = SCALE * math.log2(math.e)
NEG_INF = float("-inf")


def dot_t(a, b):
    return lax.dot_general(a, b, (((1,), (1,)), ((), ())), preferred_element_type=jnp.float32)


def dot(a, b):
    return lax.dot_general(a, b, (((1,), (0,)), ((), ())), preferred_element_type=jnp.float32)


def dot_lead(a, b):
    return lax.dot_general(a, b, (((0,), (0,)), ((), ())), preferred_element_type=jnp.float32)


def far_place(clip, index, clips, count, ends_apart):
    other = index + 1 if index % 2 else index - 1
    if 0 <= other < count:
        return clip * count + other
    if clips % 2 == 0 and not ends_apart:
        return (clip ^ 1) * count + index
    return clip * count + other % count


def mate_of(position):
    return position + 1 - 2 * lax.rem(position, 2)


def far_of(position):
    return position - 1 + 2 * lax.rem(position, 2)


def tile_bias(list_ref, count_ref, row_tile, key_tile):
    slots, tiles = list_ref.shape
    row = jnp.clip(row_tile, 0, tiles - 1)
    inside = row == row_tile
    hit = jnp.bool_(False)
    for j in range(slots):
        hit = hit | ((list_ref[j, row] == key_tile) & (j < count_ref[row]))
    return jnp.where(hit & inside, 0.0, NEG_INF).astype(jnp.float32)


def block_bias(list_ref, row_tile, block):
    slots, tiles = list_ref.shape
    row = jnp.clip(row_tile, 0, tiles - 1)
    inside = row == row_tile
    hit = jnp.bool_(False)
    for j in range(slots):
        hit = hit | (list_ref[j, row] == block)
    return jnp.where(hit & inside, 0.0, NEG_INF).astype(jnp.float32)


def lanes_of(first, second):
    lane = lax.broadcasted_iota(jnp.int32, (1, 2 * TILE), 1)
    return jnp.where(lane < TILE, first, second)


def own_video_rows(list_ref, count_ref, position):
    rows = []
    for holder in (position, mate_of(position), far_of(position)):
        for w in range(2):
            key_tile = 2 * holder + w
            rows.append(
                lanes_of(
                    tile_bias(list_ref, count_ref, 2 * position, key_tile),
                    tile_bias(list_ref, count_ref, 2 * position + 1, key_tile),
                )
            )
    return rows


def own_audio_rows(list_ref, position):
    rows = []
    for block in (position, mate_of(position), far_of(position)):
        rows.append(
            lanes_of(
                block_bias(list_ref, 2 * position, block),
                block_bias(list_ref, 2 * position + 1, block),
            )
        )
    return rows


def masked(scores, rows, height):
    return jnp.concatenate(
        [scores[i * height : (i + 1) * height] * SCORE_FACTOR + row for i, row in enumerate(rows)],
        axis=0,
    )


def softmax_cols(scores):
    top = jnp.max(scores, axis=0, keepdims=True)
    grown = jnp.exp2(scores - top)
    total = jnp.sum(grown, axis=0, keepdims=True)
    return grown * (1.0 / total), top + jnp.log2(total)


def head_cols(ref):
    return [slice(i, i + HEAD_DIM) for i in range(0, ref.shape[1], HEAD_DIM)]


def rows_at(refs, first, count, cols):
    return jnp.concatenate([ref[first : first + count, cols] for ref in refs], axis=0)


def gated_by(gate, cotangent):
    return (gate * cotangent.astype(jnp.float32)).astype(jnp.bfloat16)


def gate_kernel(position_ref, audio_list, q_ref, do_ref, a0, a1, a2, gate_out):
    rows = own_audio_rows(audio_list, position_ref[0])
    block = a0.shape[0] // 2
    heads = head_cols(q_ref)
    raw = [dot_t(rows_at((a0, a1, a2), 0, block, c), q_ref[:, c]) for c in heads]
    weights = [softmax_cols(masked(r, rows, block))[0].astype(jnp.bfloat16) for r in raw]
    spread = [dot(w, do_ref[:, c]) for w, c in zip(weights, heads)]
    for t, c in zip(spread, heads):
        values = rows_at((a0, a1, a2), block, block, c).astype(jnp.float32)
        gate_out[:, c] = jnp.sum(t * values, axis=0, keepdims=True)


def own_kernel(
    position_ref,
    tile_list,
    tile_count,
    audio_list,
    q_ref,
    do_ref,
    kv0,
    kv1,
    kv2,
    a0,
    a1,
    a2,
    gate_ref,
    dq_out,
    own_out,
    mate_k_out,
    mate_v_out,
    stat_out,
):
    position = position_ref[0]
    video_rows = own_video_rows(tile_list, tile_count, position)
    audio_rows = own_audio_rows(audio_list, position)
    own = kv0.shape[0] // 2
    window = 3 * own
    block = a0.shape[0] // 2
    video, audio = (kv0, kv1, kv2), (a0, a1, a2)
    heads = head_cols(q_ref)
    products = []
    for c in heads:
        q = q_ref[:, c]
        do = do_ref[:, c]
        keys = jnp.concatenate([rows_at(video, 0, own, c), rows_at(audio, 0, block, c)], axis=0)
        raw = dot_t(keys, q)
        video_dp = dot_t(rows_at(video, own, own, c), do)
        cross_dp = dot_t(rows_at(audio, block, block, c), gated_by(gate_ref[:, c], do))
        products.append((raw, video_dp, cross_dp))
    grads = []
    for h, (raw, video_dp, cross_dp) in enumerate(products):
        video_prob, video_total = softmax_cols(masked(raw[:window], video_rows, TILE))
        cross_prob, cross_total = softmax_cols(masked(raw[window:], audio_rows, block))
        video_weights = video_prob.astype(jnp.bfloat16)
        cross_weights = cross_prob.astype(jnp.bfloat16)
        video_delta = jnp.sum(video_weights.astype(jnp.float32) * video_dp, axis=0, keepdims=True)
        cross_delta = jnp.sum(cross_weights.astype(jnp.float32) * cross_dp, axis=0, keepdims=True)
        video_ds = (video_prob * (video_dp - video_delta)).astype(jnp.bfloat16)
        cross_ds = (cross_prob * (cross_dp - cross_delta)).astype(jnp.bfloat16)
        stat_out[4 * h : 4 * h + 4, :] = jnp.concatenate(
            [video_total, video_delta, cross_total, cross_delta], axis=0
        )
        grads.append((video_ds, cross_ds, video_weights[: 2 * own], cross_weights[: 2 * block]))
    for c, (video_ds, cross_ds, video_weights, cross_weights) in zip(heads, grads):
        q = q_ref[:, c]
        do = do_ref[:, c]
        keys = jnp.concatenate([rows_at(video, 0, own, c), rows_at(audio, 0, block, c)], axis=0)
        both_ds = jnp.concatenate([video_ds, cross_ds], axis=0)
        dq_out[:, c] = (dot_lead(both_ds, keys) * SCALE).astype(jnp.bfloat16)
        dk = dot(video_ds[: 2 * own], q)
        dv = dot(video_weights, do)
        dak = dot(cross_ds[: 2 * block], q)
        dav = dot(cross_weights, gated_by(gate_ref[:, c], do))
        own_out[:own, c] = dk[:own]
        own_out[own : 2 * own, c] = dv[:own]
        own_out[2 * own : 2 * own + block, c] = dak[:block]
        own_out[2 * own + block :, c] = dav[:block]
        mate_k_out[:own, c] = dk[own:].astype(jnp.bfloat16)
        mate_k_out[own:, c] = dak[block:].astype(jnp.bfloat16)
        mate_v_out[:own, c] = dv[own:].astype(jnp.bfloat16)
        mate_v_out[own:, c] = dav[block:].astype(jnp.bfloat16)


def far_kernel(
    position_ref,
    tile_list,
    tile_count,
    audio_list,
    qo_ref,
    stat_ref,
    kv_ref,
    a_ref,
    gate_ref,
    own_in,
    mate_k_in,
    mate_v_in,
    dk_out,
    dv_out,
    dak_out,
    dav_out,
):
    position = position_ref[0]
    beside = far_of(position)
    video_rows = [
        lanes_of(
            tile_bias(tile_list, tile_count, 2 * beside, 2 * position + w),
            tile_bias(tile_list, tile_count, 2 * beside + 1, 2 * position + w),
        )
        for w in range(2)
    ]
    audio_row = lanes_of(
        block_bias(audio_list, 2 * beside, position),
        block_bias(audio_list, 2 * beside + 1, position),
    )
    own = kv_ref.shape[0] // 2
    block = a_ref.shape[0] // 2
    heads = head_cols(kv_ref)
    products = []
    for c in heads:
        q = qo_ref[:own, c]
        do = qo_ref[own:, c]
        keys = jnp.concatenate([kv_ref[:own, c], a_ref[:block, c]], axis=0)
        products.append(
            (
                dot_t(keys, q),
                dot_t(kv_ref[own:, c], do),
                dot_t(a_ref[block:, c], gated_by(gate_ref[:, c], do)),
            )
        )
    grads = []
    for h, (raw, video_dp, cross_dp) in enumerate(products):
        stats = stat_ref[4 * h : 4 * h + 4, :]
        video_prob = jnp.exp2(masked(raw[:own], video_rows, TILE) - stats[0:1])
        cross_prob = jnp.exp2(raw[own:] * SCORE_FACTOR + audio_row - stats[2:3])
        video_ds = (video_prob * (video_dp - stats[1:2])).astype(jnp.bfloat16)
        cross_ds = (cross_prob * (cross_dp - stats[3:4])).astype(jnp.bfloat16)
        grads.append(
            (
                jnp.concatenate([video_ds, cross_ds], axis=0),
                video_prob.astype(jnp.bfloat16),
                cross_prob.astype(jnp.bfloat16),
            )
        )
    for c, (both_ds, video_weights, cross_weights) in zip(heads, grads):
        q = qo_ref[:own, c]
        do = qo_ref[own:, c]
        from_q = dot(both_ds, q)
        from_do = dot(video_weights, do)
        from_gated = dot(cross_weights, gated_by(gate_ref[:, c], do))
        mate_k = mate_k_in[:, c].astype(jnp.float32)
        mate_v = mate_v_in[:, c].astype(jnp.float32)
        sums = own_in[:, c]
        audio = sums[2 * own :]
        dk_out[:, c] = ((sums[:own] + mate_k[:own] + from_q[:own]) * SCALE).astype(dk_out.dtype)
        dv_out[:, c] = (sums[own : 2 * own] + mate_v[:own] + from_do).astype(dv_out.dtype)
        dak_out[:, c] = ((audio[:block] + mate_k[own:] + from_q[own:]) * SCALE).astype(dak_out.dtype)
        dav_out[:, c] = (audio[block:] + mate_v[own:] + from_gated).astype(dav_out.dtype)


def heads_per_step(heads, most):
    return max(g for g in range(1, most + 1) if heads % g == 0)


def flipped(part, axis, bit, bits=2):
    size = lax.axis_size(axis)
    flips = [f * bit for f in range(1, 2**bits) if f * bit < size]
    return [part] + [lax.ppermute(part, axis, [(i, i ^ f) for i in range(size)]) for f in flips]


def flipped_apart(part):
    size = lax.axis_size("ctx")
    return [
        lax.ppermute(part, "ctx", [(i, i ^ (step + 8 * (i % 2))) for i in range(size)])
        for step in (0, 2, 4, 6)
    ]


def joined(parts):
    if len(parts) < 4:
        return sum(parts[1:], parts[0])
    return (parts[0] + parts[1]) + (parts[2] + parts[3])


def after(first, then):
    return lax.optimization_barrier((first, then))


SMEM = pl.BlockSpec(memory_space=pltpu.SMEM)


def cols_spec(rows, width):
    return pl.BlockSpec((rows, width), lambda i: (0, i))


def cost(flops, arrays):
    return pl.CostEstimate(
        flops=flops,
        bytes_accessed=0,
        transcendentals=0,
    )


def per_device(
    video_query,
    video_key,
    video_value,
    audio_key,
    audio_value,
    cross_gate,
    out_cotangent,
    tile_list,
    tile_count,
    audio_list,
):
    clips, rows, width = video_query.shape
    block = audio_key.shape[1]
    heads = width // HEAD_DIM
    count = lax.axis_size("ctx")
    position = lax.axis_index("ctx").astype(jnp.int32).reshape(1)
    mate_pairs = [(i, i ^ 1) for i in range(count)]
    clip_places = lax.axis_size("dp")

    def to_mate(x):
        return lax.ppermute(x, "ctx", mate_pairs)

    def to_far(x, ends_apart):
        pairs = [
            (c * count + i, far_place(c, i, clip_places, count, ends_apart))
            for c in range(clip_places)
            for i in range(count)
        ]
        return lax.ppermute(x, ("dp", "ctx"), pairs)

    q, k, v, do = (x.reshape(rows, width) for x in (video_query, video_key, video_value, out_cotangent))
    ak, av = (x.reshape(block, width) for x in (audio_key, audio_value))
    gate = cross_gate.reshape(1, width)
    tile_list, audio_list = tile_list.T, audio_list.T

    a = jnp.concatenate([ak, av], axis=0)
    kv = jnp.concatenate([k, v], axis=0)
    kv, a = after(kv, a)
    a_far, a_mate = to_far(a, False), to_mate(a)
    kv_far, kv_mate = to_far(kv, False), to_mate(kv)

    f32, bf16 = jnp.float32, jnp.bfloat16

    def specs(group):
        step = group * HEAD_DIM
        return (
            (heads // group,),
            cols_spec(2 * rows, step),
            cols_spec(rows, step),
            cols_spec(2 * block, step),
            cols_spec(block, step),
            cols_spec(1, step),
            pl.BlockSpec((4 * group, rows), lambda i: (i, 0)),
        )

    def array(n, dtype):
        return jax.ShapeDtypeStruct((n, width), dtype)

    params = pltpu.CompilerParams(vmem_limit_bytes=24 * 2**20)

    grid, pair, vspec, apair, aspec, gspec, sspec = specs(heads_per_step(heads, 24))
    gate_args = (q, do, a, a_mate, a_far)
    gate_part = pl.pallas_call(
        gate_kernel,
        grid=grid,
        in_specs=[SMEM, SMEM] + [vspec] * 2 + [apair] * 3,
        out_specs=gspec,
        out_shape=array(1, f32),
        cost_estimate=cost(20_000_000_000, gate_args),
        compiler_params=params,
        name="gate_terms",
    )(position, audio_list, *gate_args)

    total = joined(flipped(gate_part, "ctx", 1, 1))
    kv_mate, total = after(kv_mate, total)
    parts = flipped_apart(total)
    kv_far, parts = after(kv_far, parts)
    parts, q_next = after(parts, q)
    qo_far = to_far(jnp.concatenate([q_next, do], axis=0), True)
    parts = flipped(joined(parts), "dp", 1)

    grid, pair, vspec, apair, aspec, gspec, sspec = specs(heads_per_step(heads, 8))
    sums_spec = cols_spec(2 * (rows + block), vspec.block_shape[1])
    half_spec = cols_spec(rows + block, vspec.block_shape[1])
    own_args = (q, do, kv, kv_mate, kv_far, a, a_mate, a_far)
    dq, own_sums, mate_k, mate_v, stats = pl.pallas_call(
        own_kernel,
        grid=grid,
        in_specs=[SMEM] * 4 + [vspec] * 2 + [pair] * 3 + [apair] * 3 + [gspec],
        out_specs=[vspec, sums_spec, half_spec, half_spec, sspec],
        out_shape=[
            array(rows, bf16),
            array(2 * (rows + block), f32),
            array(rows + block, bf16),
            array(rows + block, bf16),
            jax.ShapeDtypeStruct((4 * heads, rows), f32),
        ],
        cost_estimate=cost(0_000_000_000, own_args),
        compiler_params=params,
        name="own_queries",
    )(position, tile_list, tile_count, audio_list, *own_args, gate)

    (stats, mate_k, mate_v), parts = after((stats, mate_k, mate_v), parts)
    stats_far = to_far(stats, True)
    mate_k, mate_v = to_mate(mate_k), to_mate(mate_v)
    total = joined(flipped(joined(parts), "ctx", 1, 1))
    (mate_k, mate_v), total = after((mate_k, mate_v), total)
    parts = flipped(total, "ctx", 16)

    far_args = (qo_far, stats_far, kv, a, gate, own_sums, mate_k, mate_v)
    dk, dv, dak, dav = pl.pallas_call(
        far_kernel,
        grid=grid,
        in_specs=[SMEM] * 4 + [pair, sspec, pair, apair, gspec, sums_spec, half_spec, half_spec],
        out_specs=[vspec, vspec, aspec, aspec],
        out_shape=[array(rows, bf16), array(rows, bf16), array(block, bf16), array(block, bf16)],
        cost_estimate=cost(5_000_000_000, far_args),
        compiler_params=params,
        name="far_queries",
    )(position, tile_list, tile_count, audio_list, *far_args)

    dak, parts = after(dak, parts)
    total = joined(parts)

    return (
        dq.reshape(clips, rows, width),
        dk.reshape(clips, rows, width),
        dv.reshape(clips, rows, width),
        dak.reshape(clips, block, width),
        dav.reshape(clips, block, width),
        total.reshape(width),
    )


def solution(mesh):
    placed = P("dp", "ctx", None)
    return jax.shard_map(
        per_device,
        mesh=mesh,
        in_specs=(placed,) * 5 + (P(), placed, P(), P(), P()),
        out_specs=(placed,) * 5 + (P(),),
        check_vma=False,
    )
```

```python
import math

import jax
import jax.numpy as jnp
from jax import lax
from jax.experimental import pallas as pl
from jax.experimental.pallas import tpu as pltpu
from jax.sharding import PartitionSpec as P

HEAD_DIM = 128
TILE = 64
SCALE = 1.0 / math.sqrt(HEAD_DIM)
SCORE_FACTOR = SCALE * math.log2(math.e)
NEG_INF = float("-inf")


def dot_t(a, b):
    return lax.dot_general(a, b, (((1,), (1,)), ((), ())), preferred_element_type=jnp.float32)


def dot(a, b):
    return lax.dot_general(a, b, (((1,), (0,)), ((), ())), preferred_element_type=jnp.float32)


def dot_lead(a, b):
    return lax.dot_general(a, b, (((0,), (0,)), ((), ())), preferred_element_type=jnp.float32)


def far_place(clip, index, clips, count, ends_apart):
    other = index + 1 if index % 2 else index - 1
    if 0 <= other < count:
        return clip * count + other
    if clips % 2 == 0 and not ends_apart:
        return (clip ^ 1) * count + index
    return clip * count + other % count


def mate_of(position):
    return position + 1 - 2 * lax.rem(position, 2)


def far_of(position):
    return position - 1 + 2 * lax.rem(position, 2)


def tile_bias(list_ref, count_ref, row_tile, key_tile):
    slots, tiles = list_ref.shape
    row = jnp.clip(row_tile, 0, tiles - 1)
    inside = row == row_tile
    hit = jnp.bool_(False)
    for j in range(slots):
        hit = hit | ((list_ref[j, row] == key_tile) & (j < count_ref[row]))
    return jnp.where(hit & inside, 0.0, NEG_INF).astype(jnp.float32)


def block_bias(list_ref, row_tile, block):
    slots, tiles = list_ref.shape
    row = jnp.clip(row_tile, 0, tiles - 1)
    inside = row == row_tile
    hit = jnp.bool_(False)
    for j in range(slots):
        hit = hit | (list_ref[j, row] == block)
    return jnp.where(hit & inside, 0.0, NEG_INF).astype(jnp.float32)


def lanes_of(first, second):
    lane = lax.broadcasted_iota(jnp.int32, (1, 2 * TILE), 1)
    return jnp.where(lane < TILE, first, second)


def own_video_rows(list_ref, count_ref, position):
    rows = []
    for holder in (position, mate_of(position), far_of(position)):
        for w in range(2):
            key_tile = 2 * holder + w
            rows.append(
                lanes_of(
                    tile_bias(list_ref, count_ref, 2 * position, key_tile),
                    tile_bias(list_ref, count_ref, 2 * position + 1, key_tile),
                )
            )
    return rows


def own_audio_rows(list_ref, position):
    rows = []
    for block in (position, mate_of(position), far_of(position)):
        rows.append(
            lanes_of(
                block_bias(list_ref, 2 * position, block),
                block_bias(list_ref, 2 * position + 1, block),
            )
        )
    return rows


def masked(scores, rows, height):
    return jnp.concatenate(
        [scores[i * height : (i + 1) * height] * SCORE_FACTOR + row for i, row in enumerate(rows)],
        axis=0,
    )


def softmax_cols(scores):
    top = jnp.max(scores, axis=0, keepdims=True)
    grown = jnp.exp2(scores - top)
    total = jnp.sum(grown, axis=0, keepdims=True)
    return grown * (1.0 / total), top + jnp.log2(total)


def head_cols(ref):
    return [slice(i, i + HEAD_DIM) for i in range(0, ref.shape[1], HEAD_DIM)]


def rows_at(refs, first, count, cols):
    return jnp.concatenate([ref[first : first + count, cols] for ref in refs], axis=0)


def gated_by(gate, cotangent):
    return (gate * cotangent.astype(jnp.float32)).astype(jnp.bfloat16)


def gate_kernel(position_ref, audio_list, q_ref, do_ref, a0, a1, a2, gate_out):
    rows = own_audio_rows(audio_list, position_ref[0])
    block = a0.shape[0] // 2
    heads = head_cols(q_ref)
    raw = [dot_t(rows_at((a0, a1, a2), 0, block, c), q_ref[:, c]) for c in heads]
    weights = [softmax_cols(masked(r, rows, block))[0].astype(jnp.bfloat16) for r in raw]
    spread = [dot(w, do_ref[:, c]) for w, c in zip(weights, heads)]
    for t, c in zip(spread, heads):
        values = rows_at((a0, a1, a2), block, block, c).astype(jnp.float32)
        gate_out[:, c] = jnp.sum(t * values, axis=0, keepdims=True)


def own_kernel(
    position_ref,
    tile_list,
    tile_count,
    audio_list,
    q_ref,
    do_ref,
    kv0,
    kv1,
    kv2,
    a0,
    a1,
    a2,
    gate_ref,
    dq_out,
    own_out,
    mate_k_out,
    mate_v_out,
    stat_out,
):
    position = position_ref[0]
    video_rows = own_video_rows(tile_list, tile_count, position)
    audio_rows = own_audio_rows(audio_list, position)
    own = kv0.shape[0] // 2
    window = 3 * own
    block = a0.shape[0] // 2
    video, audio = (kv0, kv1, kv2), (a0, a1, a2)
    heads = head_cols(q_ref)
    products = []
    for c in heads:
        q = q_ref[:, c]
        do = do_ref[:, c]
        keys = jnp.concatenate([rows_at(video, 0, own, c), rows_at(audio, 0, block, c)], axis=0)
        raw = dot_t(keys, q)
        video_dp = dot_t(rows_at(video, own, own, c), do)
        cross_dp = dot_t(rows_at(audio, block, block, c), gated_by(gate_ref[:, c], do))
        products.append((raw, video_dp, cross_dp))
    grads = []
    for h, (raw, video_dp, cross_dp) in enumerate(products):
        video_prob, video_total = softmax_cols(masked(raw[:window], video_rows, TILE))
        cross_prob, cross_total = softmax_cols(masked(raw[window:], audio_rows, block))
        video_weights = video_prob.astype(jnp.bfloat16)
        cross_weights = cross_prob.astype(jnp.bfloat16)
        video_delta = jnp.sum(video_weights.astype(jnp.float32) * video_dp, axis=0, keepdims=True)
        cross_delta = jnp.sum(cross_weights.astype(jnp.float32) * cross_dp, axis=0, keepdims=True)
        video_ds = (video_prob * (video_dp - video_delta)).astype(jnp.bfloat16)
        cross_ds = (cross_prob * (cross_dp - cross_delta)).astype(jnp.bfloat16)
        stat_out[4 * h : 4 * h + 4, :] = jnp.concatenate(
            [video_total, video_delta, cross_total, cross_delta], axis=0
        )
        grads.append((video_ds, cross_ds, video_weights[: 2 * own], cross_weights[: 2 * block]))
    for c, (video_ds, cross_ds, video_weights, cross_weights) in zip(heads, grads):
        q = q_ref[:, c]
        do = do_ref[:, c]
        keys = jnp.concatenate([rows_at(video, 0, own, c), rows_at(audio, 0, block, c)], axis=0)
        both_ds = jnp.concatenate([video_ds, cross_ds], axis=0)
        dq_out[:, c] = (dot_lead(both_ds, keys) * SCALE).astype(jnp.bfloat16)
        dk = dot(video_ds[: 2 * own], q)
        dv = dot(video_weights, do)
        dak = dot(cross_ds[: 2 * block], q)
        dav = dot(cross_weights, gated_by(gate_ref[:, c], do))
        own_out[:own, c] = dk[:own]
        own_out[own : 2 * own, c] = dv[:own]
        own_out[2 * own : 2 * own + block, c] = dak[:block]
        own_out[2 * own + block :, c] = dav[:block]
        mate_k_out[:own, c] = dk[own:].astype(jnp.bfloat16)
        mate_k_out[own:, c] = dak[block:].astype(jnp.bfloat16)
        mate_v_out[:own, c] = dv[own:].astype(jnp.bfloat16)
        mate_v_out[own:, c] = dav[block:].astype(jnp.bfloat16)


def far_kernel(
    position_ref,
    tile_list,
    tile_count,
    audio_list,
    qo_ref,
    stat_ref,
    kv_ref,
    a_ref,
    gate_ref,
    own_in,
    mate_k_in,
    mate_v_in,
    dk_out,
    dv_out,
    dak_out,
    dav_out,
):
    position = position_ref[0]
    beside = far_of(position)
    video_rows = [
        lanes_of(
            tile_bias(tile_list, tile_count, 2 * beside, 2 * position + w),
            tile_bias(tile_list, tile_count, 2 * beside + 1, 2 * position + w),
        )
        for w in range(2)
    ]
    audio_row = lanes_of(
        block_bias(audio_list, 2 * beside, position),
        block_bias(audio_list, 2 * beside + 1, position),
    )
    own = kv_ref.shape[0] // 2
    block = a_ref.shape[0] // 2
    heads = head_cols(kv_ref)
    products = []
    for c in heads:
        q = qo_ref[:own, c]
        do = qo_ref[own:, c]
        keys = jnp.concatenate([kv_ref[:own, c], a_ref[:block, c]], axis=0)
        products.append(
            (
                dot_t(keys, q),
                dot_t(kv_ref[own:, c], do),
                dot_t(a_ref[block:, c], gated_by(gate_ref[:, c], do)),
            )
        )
    grads = []
    for h, (raw, video_dp, cross_dp) in enumerate(products):
        stats = stat_ref[4 * h : 4 * h + 4, :]
        video_prob = jnp.exp2(masked(raw[:own], video_rows, TILE) - stats[0:1])
        cross_prob = jnp.exp2(raw[own:] * SCORE_FACTOR + audio_row - stats[2:3])
        video_ds = (video_prob * (video_dp - stats[1:2])).astype(jnp.bfloat16)
        cross_ds = (cross_prob * (cross_dp - stats[3:4])).astype(jnp.bfloat16)
        grads.append(
            (
                jnp.concatenate([video_ds, cross_ds], axis=0),
                video_prob.astype(jnp.bfloat16),
                cross_prob.astype(jnp.bfloat16),
            )
        )
    for c, (both_ds, video_weights, cross_weights) in zip(heads, grads):
        q = qo_ref[:own, c]
        do = qo_ref[own:, c]
        from_q = dot(both_ds, q)
        from_do = dot(video_weights, do)
        from_gated = dot(cross_weights, gated_by(gate_ref[:, c], do))
        mate_k = mate_k_in[:, c].astype(jnp.float32)
        mate_v = mate_v_in[:, c].astype(jnp.float32)
        sums = own_in[:, c]
        audio = sums[2 * own :]
        dk_out[:, c] = ((sums[:own] + mate_k[:own] + from_q[:own]) * SCALE).astype(dk_out.dtype)
        dv_out[:, c] = (sums[own : 2 * own] + mate_v[:own] + from_do).astype(dv_out.dtype)
        dak_out[:, c] = ((audio[:block] + mate_k[own:] + from_q[own:]) * SCALE).astype(dak_out.dtype)
        dav_out[:, c] = (audio[block:] + mate_v[own:] + from_gated).astype(dav_out.dtype)


def heads_per_step(heads, most):
    return max(g for g in range(1, most + 1) if heads % g == 0)


def flipped(part, axis, bit, bits=2):
    size = lax.axis_size(axis)
    flips = [f * bit for f in range(1, 2**bits) if f * bit < size]
    return [part] + [lax.ppermute(part, axis, [(i, i ^ f) for i in range(size)]) for f in flips]


def flipped_apart(part):
    size = lax.axis_size("ctx")
    return [
        lax.ppermute(part, "ctx", [(i, i ^ (step + 8 * (i % 2))) for i in range(size)])
        for step in (0, 2, 4, 6)
    ]


def joined(parts):
    if len(parts) < 4:
        return sum(parts[1:], parts[0])
    return (parts[0] + parts[1]) + (parts[2] + parts[3])


def after(first, then):
    return lax.optimization_barrier((first, then))


SMEM = pl.BlockSpec(memory_space=pltpu.SMEM)


def cols_spec(rows, width):
    return pl.BlockSpec((rows, width), lambda i: (0, i))


def cost(flops, arrays):
    return pl.CostEstimate(
        flops=flops,
        bytes_accessed=0,
        transcendentals=0,
    )


def per_device(
    video_query,
    video_key,
    video_value,
    audio_key,
    audio_value,
    cross_gate,
    out_cotangent,
    tile_list,
    tile_count,
    audio_list,
):
    clips, rows, width = video_query.shape
    block = audio_key.shape[1]
    heads = width // HEAD_DIM
    count = lax.axis_size("ctx")
    position = lax.axis_index("ctx").astype(jnp.int32).reshape(1)
    mate_pairs = [(i, i ^ 1) for i in range(count)]
    clip_places = lax.axis_size("dp")

    def to_mate(x):
        return lax.ppermute(x, "ctx", mate_pairs)

    def to_far(x, ends_apart):
        pairs = [
            (c * count + i, far_place(c, i, clip_places, count, ends_apart))
            for c in range(clip_places)
            for i in range(count)
        ]
        return lax.ppermute(x, ("dp", "ctx"), pairs)

    q, k, v, do = (x.reshape(rows, width) for x in (video_query, video_key, video_value, out_cotangent))
    ak, av = (x.reshape(block, width) for x in (audio_key, audio_value))
    gate = cross_gate.reshape(1, width)
    tile_list, audio_list = tile_list.T, audio_list.T

    a = jnp.concatenate([ak, av], axis=0)
    kv = jnp.concatenate([k, v], axis=0)
    kv, a = after(kv, a)
    a_far, a_mate = to_far(a, False), to_mate(a)
    kv_far, kv_mate = to_far(kv, False), to_mate(kv)

    f32, bf16 = jnp.float32, jnp.bfloat16

    def specs(group):
        step = group * HEAD_DIM
        return (
            (heads // group,),
            cols_spec(2 * rows, step),
            cols_spec(rows, step),
            cols_spec(2 * block, step),
            cols_spec(block, step),
            cols_spec(1, step),
            pl.BlockSpec((4 * group, rows), lambda i: (i, 0)),
        )

    def array(n, dtype):
        return jax.ShapeDtypeStruct((n, width), dtype)

    params = pltpu.CompilerParams(vmem_limit_bytes=32 * 2**20)

    grid, pair, vspec, apair, aspec, gspec, sspec = specs(heads_per_step(heads, 24))
    gate_args = (q, do, a, a_mate, a_far)
    gate_part = pl.pallas_call(
        gate_kernel,
        grid=grid,
        in_specs=[SMEM, SMEM] + [vspec] * 2 + [apair] * 3,
        out_specs=gspec,
        out_shape=array(1, f32),
        cost_estimate=cost(20_000_000_000, gate_args),
        compiler_params=params,
        name="gate_terms",
    )(position, audio_list, *gate_args)

    total = joined(flipped(gate_part, "ctx", 1, 1))
    kv_mate, total = after(kv_mate, total)
    parts = flipped_apart(total)
    kv_far, parts = after(kv_far, parts)
    parts, q_next = after(parts, q)
    qo_far = to_far(jnp.concatenate([q_next, do], axis=0), True)
    parts = flipped(joined(parts), "dp", 1)

    grid, pair, vspec, apair, aspec, gspec, sspec = specs(heads_per_step(heads, 12))
    sums_spec = cols_spec(2 * (rows + block), vspec.block_shape[1])
    half_spec = cols_spec(rows + block, vspec.block_shape[1])
    own_args = (q, do, kv, kv_mate, kv_far, a, a_mate, a_far)
    dq, own_sums, mate_k, mate_v, stats = pl.pallas_call(
        own_kernel,
        grid=grid,
        in_specs=[SMEM] * 4 + [vspec] * 2 + [pair] * 3 + [apair] * 3 + [gspec],
        out_specs=[vspec, sums_spec, half_spec, half_spec, sspec],
        out_shape=[
            array(rows, bf16),
            array(2 * (rows + block), f32),
            array(rows + block, bf16),
            array(rows + block, bf16),
            jax.ShapeDtypeStruct((4 * heads, rows), f32),
        ],
        cost_estimate=cost(0_000_000_000, own_args),
        compiler_params=params,
        name="own_queries",
    )(position, tile_list, tile_count, audio_list, *own_args, gate)

    (stats, mate_k, mate_v), parts = after((stats, mate_k, mate_v), parts)
    stats_far = to_far(stats, True)
    mate_k, mate_v = to_mate(mate_k), to_mate(mate_v)
    total = joined(flipped(joined(parts), "ctx", 1, 1))
    (mate_k, mate_v), total = after((mate_k, mate_v), total)
    parts = flipped(total, "ctx", 16)

    far_args = (qo_far, stats_far, kv, a, gate, own_sums, mate_k, mate_v)
    dk, dv, dak, dav = pl.pallas_call(
        far_kernel,
        grid=grid,
        in_specs=[SMEM] * 4 + [pair, sspec, pair, apair, gspec, sums_spec, half_spec, half_spec],
        out_specs=[vspec, vspec, aspec, aspec],
        out_shape=[array(rows, bf16), array(rows, bf16), array(block, bf16), array(block, bf16)],
        cost_estimate=cost(5_000_000_000, far_args),
        compiler_params=params,
        name="far_queries",
    )(position, tile_list, tile_count, audio_list, *far_args)

    dak, parts = after(dak, parts)
    total = joined(parts)

    return (
        dq.reshape(clips, rows, width),
        dk.reshape(clips, rows, width),
        dv.reshape(clips, rows, width),
        dak.reshape(clips, block, width),
        dav.reshape(clips, block, width),
        total.reshape(width),
    )


def solution(mesh):
    placed = P("dp", "ctx", None)
    return jax.shard_map(
        per_device,
        mesh=mesh,
        in_specs=(placed,) * 5 + (P(), placed, P(), P(), P()),
        out_specs=(placed,) * 5 + (P(),),
        check_vma=False,
    )
```

```python
import math

import jax
import jax.numpy as jnp
from jax import lax
from jax.experimental import pallas as pl
from jax.experimental.pallas import tpu as pltpu
from jax.sharding import PartitionSpec as P

HEAD_DIM = 128
TILE = 64
SCALE = 1.0 / math.sqrt(HEAD_DIM)
SCORE_FACTOR = SCALE * math.log2(math.e)
NEG_INF = float("-inf")


def dot_t(a, b):
    return lax.dot_general(a, b, (((1,), (1,)), ((), ())), preferred_element_type=jnp.float32)


def dot(a, b):
    return lax.dot_general(a, b, (((1,), (0,)), ((), ())), preferred_element_type=jnp.float32)


def dot_lead(a, b):
    return lax.dot_general(a, b, (((0,), (0,)), ((), ())), preferred_element_type=jnp.float32)


def far_place(clip, index, clips, count, ends_apart):
    other = index + 1 if index % 2 else index - 1
    if 0 <= other < count:
        return clip * count + other
    if clips % 2 == 0 and not ends_apart:
        return (clip ^ 1) * count + index
    return clip * count + other % count


def mate_of(position):
    return position + 1 - 2 * lax.rem(position, 2)


def far_of(position):
    return position - 1 + 2 * lax.rem(position, 2)


def tile_bias(list_ref, count_ref, row_tile, key_tile):
    slots, tiles = list_ref.shape
    row = jnp.clip(row_tile, 0, tiles - 1)
    inside = row == row_tile
    hit = jnp.bool_(False)
    for j in range(slots):
        hit = hit | ((list_ref[j, row] == key_tile) & (j < count_ref[row]))
    return jnp.where(hit & inside, 0.0, NEG_INF).astype(jnp.float32)


def block_bias(list_ref, row_tile, block):
    slots, tiles = list_ref.shape
    row = jnp.clip(row_tile, 0, tiles - 1)
    inside = row == row_tile
    hit = jnp.bool_(False)
    for j in range(slots):
        hit = hit | (list_ref[j, row] == block)
    return jnp.where(hit & inside, 0.0, NEG_INF).astype(jnp.float32)


def lanes_of(first, second):
    lane = lax.broadcasted_iota(jnp.int32, (1, 2 * TILE), 1)
    return jnp.where(lane < TILE, first, second)


def own_video_rows(list_ref, count_ref, position):
    rows = []
    for holder in (position, mate_of(position), far_of(position)):
        for w in range(2):
            key_tile = 2 * holder + w
            rows.append(
                lanes_of(
                    tile_bias(list_ref, count_ref, 2 * position, key_tile),
                    tile_bias(list_ref, count_ref, 2 * position + 1, key_tile),
                )
            )
    return rows


def own_audio_rows(list_ref, position):
    rows = []
    for block in (position, mate_of(position), far_of(position)):
        rows.append(
            lanes_of(
                block_bias(list_ref, 2 * position, block),
                block_bias(list_ref, 2 * position + 1, block),
            )
        )
    return rows


def masked(scores, rows, height):
    return jnp.concatenate(
        [scores[i * height : (i + 1) * height] * SCORE_FACTOR + row for i, row in enumerate(rows)],
        axis=0,
    )


def softmax_cols(scores):
    top = jnp.max(scores, axis=0, keepdims=True)
    grown = jnp.exp2(scores - top)
    total = jnp.sum(grown, axis=0, keepdims=True)
    return grown * (1.0 / total), top + jnp.log2(total)


def head_cols(ref):
    return [slice(i, i + HEAD_DIM) for i in range(0, ref.shape[1], HEAD_DIM)]


def rows_at(refs, first, count, cols):
    return jnp.concatenate([ref[first : first + count, cols] for ref in refs], axis=0)


def gated_by(gate, cotangent):
    return (gate * cotangent.astype(jnp.float32)).astype(jnp.bfloat16)


def gate_kernel(position_ref, audio_list, q_ref, do_ref, a0, a1, a2, gate_out):
    rows = own_audio_rows(audio_list, position_ref[0])
    block = a0.shape[0] // 2
    heads = head_cols(q_ref)
    raw = [dot_t(rows_at((a0, a1, a2), 0, block, c), q_ref[:, c]) for c in heads]
    weights = [softmax_cols(masked(r, rows, block))[0].astype(jnp.bfloat16) for r in raw]
    spread = [dot(w, do_ref[:, c]) for w, c in zip(weights, heads)]
    for t, c in zip(spread, heads):
        values = rows_at((a0, a1, a2), block, block, c).astype(jnp.float32)
        gate_out[:, c] = jnp.sum(t * values, axis=0, keepdims=True)


def own_kernel(
    position_ref,
    tile_list,
    tile_count,
    audio_list,
    q_ref,
    do_ref,
    kv0,
    kv1,
    kv2,
    a0,
    a1,
    a2,
    gate_ref,
    dq_out,
    own_out,
    mate_k_out,
    mate_v_out,
    stat_out,
):
    position = position_ref[0]
    video_rows = own_video_rows(tile_list, tile_count, position)
    audio_rows = own_audio_rows(audio_list, position)
    own = kv0.shape[0] // 2
    window = 3 * own
    block = a0.shape[0] // 2
    video, audio = (kv0, kv1, kv2), (a0, a1, a2)
    heads = head_cols(q_ref)
    products = []
    for c in heads:
        q = q_ref[:, c]
        do = do_ref[:, c]
        keys = jnp.concatenate([rows_at(video, 0, own, c), rows_at(audio, 0, block, c)], axis=0)
        raw = dot_t(keys, q)
        video_dp = dot_t(rows_at(video, own, own, c), do)
        cross_dp = dot_t(rows_at(audio, block, block, c), gated_by(gate_ref[:, c], do))
        products.append((raw, video_dp, cross_dp))
    grads = []
    for h, (raw, video_dp, cross_dp) in enumerate(products):
        video_prob, video_total = softmax_cols(masked(raw[:window], video_rows, TILE))
        cross_prob, cross_total = softmax_cols(masked(raw[window:], audio_rows, block))
        video_weights = video_prob.astype(jnp.bfloat16)
        cross_weights = cross_prob.astype(jnp.bfloat16)
        video_delta = jnp.sum(video_weights.astype(jnp.float32) * video_dp, axis=0, keepdims=True)
        cross_delta = jnp.sum(cross_weights.astype(jnp.float32) * cross_dp, axis=0, keepdims=True)
        video_ds = (video_prob * (video_dp - video_delta)).astype(jnp.bfloat16)
        cross_ds = (cross_prob * (cross_dp - cross_delta)).astype(jnp.bfloat16)
        stat_out[4 * h : 4 * h + 4, :] = jnp.concatenate(
            [video_total, video_delta, cross_total, cross_delta], axis=0
        )
        grads.append((video_ds, cross_ds, video_weights[: 2 * own], cross_weights[: 2 * block]))
    for c, (video_ds, cross_ds, video_weights, cross_weights) in zip(heads, grads):
        q = q_ref[:, c]
        do = do_ref[:, c]
        keys = jnp.concatenate([rows_at(video, 0, own, c), rows_at(audio, 0, block, c)], axis=0)
        both_ds = jnp.concatenate([video_ds, cross_ds], axis=0)
        dq_out[:, c] = (dot_lead(both_ds, keys) * SCALE).astype(jnp.bfloat16)
        from_q = dot(jnp.concatenate([video_ds[: 2 * own], cross_ds[: 2 * block]], axis=0), q)
        dk, dak = from_q[: 2 * own], from_q[2 * own :]
        dv = dot(video_weights, do)
        dav = dot(cross_weights, gated_by(gate_ref[:, c], do))
        own_out[:own, c] = dk[:own]
        own_out[own : 2 * own, c] = dv[:own]
        own_out[2 * own : 2 * own + block, c] = dak[:block]
        own_out[2 * own + block :, c] = dav[:block]
        mate_k_out[:own, c] = dk[own:].astype(jnp.bfloat16)
        mate_k_out[own:, c] = dak[block:].astype(jnp.bfloat16)
        mate_v_out[:own, c] = dv[own:].astype(jnp.bfloat16)
        mate_v_out[own:, c] = dav[block:].astype(jnp.bfloat16)


def far_kernel(
    position_ref,
    tile_list,
    tile_count,
    audio_list,
    qo_ref,
    stat_ref,
    kv_ref,
    a_ref,
    gate_ref,
    own_in,
    mate_k_in,
    mate_v_in,
    dk_out,
    dv_out,
    dak_out,
    dav_out,
):
    position = position_ref[0]
    beside = far_of(position)
    video_rows = [
        lanes_of(
            tile_bias(tile_list, tile_count, 2 * beside, 2 * position + w),
            tile_bias(tile_list, tile_count, 2 * beside + 1, 2 * position + w),
        )
        for w in range(2)
    ]
    audio_row = lanes_of(
        block_bias(audio_list, 2 * beside, position),
        block_bias(audio_list, 2 * beside + 1, position),
    )
    own = kv_ref.shape[0] // 2
    block = a_ref.shape[0] // 2
    heads = head_cols(kv_ref)
    products = []
    for c in heads:
        q = qo_ref[:own, c]
        do = qo_ref[own:, c]
        keys = jnp.concatenate([kv_ref[:own, c], a_ref[:block, c]], axis=0)
        products.append(
            (
                dot_t(keys, q),
                dot_t(kv_ref[own:, c], do),
                dot_t(a_ref[block:, c], gated_by(gate_ref[:, c], do)),
            )
        )
    grads = []
    for h, (raw, video_dp, cross_dp) in enumerate(products):
        stats = stat_ref[4 * h : 4 * h + 4, :]
        video_prob = jnp.exp2(masked(raw[:own], video_rows, TILE) - stats[0:1])
        cross_prob = jnp.exp2(raw[own:] * SCORE_FACTOR + audio_row - stats[2:3])
        video_ds = (video_prob * (video_dp - stats[1:2])).astype(jnp.bfloat16)
        cross_ds = (cross_prob * (cross_dp - stats[3:4])).astype(jnp.bfloat16)
        grads.append(
            (
                jnp.concatenate([video_ds, cross_ds], axis=0),
                video_prob.astype(jnp.bfloat16),
                cross_prob.astype(jnp.bfloat16),
            )
        )
    for c, (both_ds, video_weights, cross_weights) in zip(heads, grads):
        q = qo_ref[:own, c]
        do = qo_ref[own:, c]
        from_q = dot(both_ds, q)
        from_do = dot(video_weights, do)
        from_gated = dot(cross_weights, gated_by(gate_ref[:, c], do))
        mate_k = mate_k_in[:, c].astype(jnp.float32)
        mate_v = mate_v_in[:, c].astype(jnp.float32)
        sums = own_in[:, c]
        audio = sums[2 * own :]
        dk_out[:, c] = ((sums[:own] + mate_k[:own] + from_q[:own]) * SCALE).astype(dk_out.dtype)
        dv_out[:, c] = (sums[own : 2 * own] + mate_v[:own] + from_do).astype(dv_out.dtype)
        dak_out[:, c] = ((audio[:block] + mate_k[own:] + from_q[own:]) * SCALE).astype(dak_out.dtype)
        dav_out[:, c] = (audio[block:] + mate_v[own:] + from_gated).astype(dav_out.dtype)


def heads_per_step(heads, most):
    return max(g for g in range(1, most + 1) if heads % g == 0)


def flipped(part, axis, bit, bits=2):
    size = lax.axis_size(axis)
    flips = [f * bit for f in range(1, 2**bits) if f * bit < size]
    return [part] + [lax.ppermute(part, axis, [(i, i ^ f) for i in range(size)]) for f in flips]


def flipped_apart(part):
    size = lax.axis_size("ctx")
    return [
        lax.ppermute(part, "ctx", [(i, i ^ (step + 8 * (i % 2))) for i in range(size)])
        for step in (0, 2, 4, 6)
    ]


def joined(parts):
    if len(parts) < 4:
        return sum(parts[1:], parts[0])
    return (parts[0] + parts[1]) + (parts[2] + parts[3])


def after(first, then):
    return lax.optimization_barrier((first, then))


SMEM = pl.BlockSpec(memory_space=pltpu.SMEM)


def cols_spec(rows, width):
    return pl.BlockSpec((rows, width), lambda i: (0, i))


def cost(flops, arrays):
    return pl.CostEstimate(
        flops=flops,
        bytes_accessed=0,
        transcendentals=0,
    )


def per_device(
    video_query,
    video_key,
    video_value,
    audio_key,
    audio_value,
    cross_gate,
    out_cotangent,
    tile_list,
    tile_count,
    audio_list,
):
    clips, rows, width = video_query.shape
    block = audio_key.shape[1]
    heads = width // HEAD_DIM
    count = lax.axis_size("ctx")
    position = lax.axis_index("ctx").astype(jnp.int32).reshape(1)
    mate_pairs = [(i, i ^ 1) for i in range(count)]
    clip_places = lax.axis_size("dp")

    def to_mate(x):
        return lax.ppermute(x, "ctx", mate_pairs)

    def to_far(x, ends_apart):
        pairs = [
            (c * count + i, far_place(c, i, clip_places, count, ends_apart))
            for c in range(clip_places)
            for i in range(count)
        ]
        return lax.ppermute(x, ("dp", "ctx"), pairs)

    q, k, v, do = (x.reshape(rows, width) for x in (video_query, video_key, video_value, out_cotangent))
    ak, av = (x.reshape(block, width) for x in (audio_key, audio_value))
    gate = cross_gate.reshape(1, width)
    tile_list, audio_list = tile_list.T, audio_list.T

    a = jnp.concatenate([ak, av], axis=0)
    kv = jnp.concatenate([k, v], axis=0)
    kv, a = after(kv, a)
    a_far, a_mate = to_far(a, False), to_mate(a)
    kv_far, kv_mate = to_far(kv, False), to_mate(kv)

    f32, bf16 = jnp.float32, jnp.bfloat16

    def specs(group):
        step = group * HEAD_DIM
        return (
            (heads // group,),
            cols_spec(2 * rows, step),
            cols_spec(rows, step),
            cols_spec(2 * block, step),
            cols_spec(block, step),
            cols_spec(1, step),
            pl.BlockSpec((4 * group, rows), lambda i: (i, 0)),
        )

    def array(n, dtype):
        return jax.ShapeDtypeStruct((n, width), dtype)

    params = pltpu.CompilerParams(vmem_limit_bytes=32 * 2**20)

    grid, pair, vspec, apair, aspec, gspec, sspec = specs(heads_per_step(heads, 24))
    gate_args = (q, do, a, a_mate, a_far)
    gate_part = pl.pallas_call(
        gate_kernel,
        grid=grid,
        in_specs=[SMEM, SMEM] + [vspec] * 2 + [apair] * 3,
        out_specs=gspec,
        out_shape=array(1, f32),
        cost_estimate=cost(20_000_000_000, gate_args),
        compiler_params=params,
        name="gate_terms",
    )(position, audio_list, *gate_args)

    total = joined(flipped(gate_part, "ctx", 1, 1))
    kv_mate, total = after(kv_mate, total)
    parts = flipped_apart(total)
    kv_far, parts = after(kv_far, parts)
    parts, q_next = after(parts, q)
    qo_far = to_far(jnp.concatenate([q_next, do], axis=0), True)
    parts = flipped(joined(parts), "dp", 1)

    grid, pair, vspec, apair, aspec, gspec, sspec = specs(heads_per_step(heads, 12))
    sums_spec = cols_spec(2 * (rows + block), vspec.block_shape[1])
    half_spec = cols_spec(rows + block, vspec.block_shape[1])
    own_args = (q, do, kv, kv_mate, kv_far, a, a_mate, a_far)
    dq, own_sums, mate_k, mate_v, stats = pl.pallas_call(
        own_kernel,
        grid=grid,
        in_specs=[SMEM] * 4 + [vspec] * 2 + [pair] * 3 + [apair] * 3 + [gspec],
        out_specs=[vspec, sums_spec, half_spec, half_spec, sspec],
        out_shape=[
            array(rows, bf16),
            array(2 * (rows + block), f32),
            array(rows + block, bf16),
            array(rows + block, bf16),
            jax.ShapeDtypeStruct((4 * heads, rows), f32),
        ],
        cost_estimate=cost(0_000_000_000, own_args),
        compiler_params=params,
        name="own_queries",
    )(position, tile_list, tile_count, audio_list, *own_args, gate)

    (stats, mate_k, mate_v), parts = after((stats, mate_k, mate_v), parts)
    stats_far = to_far(stats, True)
    mate_k, mate_v = to_mate(mate_k), to_mate(mate_v)
    total = joined(flipped(joined(parts), "ctx", 1, 1))
    (mate_k, mate_v), total = after((mate_k, mate_v), total)
    parts = flipped(total, "ctx", 16)

    far_args = (qo_far, stats_far, kv, a, gate, own_sums, mate_k, mate_v)
    dk, dv, dak, dav = pl.pallas_call(
        far_kernel,
        grid=grid,
        in_specs=[SMEM] * 4 + [pair, sspec, pair, apair, gspec, sums_spec, half_spec, half_spec],
        out_specs=[vspec, vspec, aspec, aspec],
        out_shape=[array(rows, bf16), array(rows, bf16), array(block, bf16), array(block, bf16)],
        cost_estimate=cost(5_000_000_000, far_args),
        compiler_params=params,
        name="far_queries",
    )(position, tile_list, tile_count, audio_list, *far_args)

    dak, parts = after(dak, parts)
    total = joined(parts)

    return (
        dq.reshape(clips, rows, width),
        dk.reshape(clips, rows, width),
        dv.reshape(clips, rows, width),
        dak.reshape(clips, block, width),
        dav.reshape(clips, block, width),
        total.reshape(width),
    )


def solution(mesh):
    placed = P("dp", "ctx", None)
    return jax.shard_map(
        per_device,
        mesh=mesh,
        in_specs=(placed,) * 5 + (P(), placed, P(), P(), P()),
        out_specs=(placed,) * 5 + (P(),),
        check_vma=False,
    )
```
